512 devices in a mesh: dp: 32 (over x_hi, z, core), tensor: 16 (over x_lo, y).
Axes of the slice: x: 4 (x_hi: 2, x_lo: 2; x = x_hi * 2 + x_lo), y: 8, z: 8, core: 2. Of those that a mesh axis runs over, the one named last changes fastest.
Arguments:
- weight: bfloat16 [7168, 18432], P('dp', 'tensor'), may hold values from -0.015625 to 0.015625
- gradient: bfloat16 [7168, 18432], P('dp', 'tensor'), may hold values from -6 to 6
- momentum: float32 [7168, 18432], P('dp', 'tensor'), may hold values from -6 to 6
- basis: float32 [7168, 512], P('dp'), may hold values from -0.0625 to 0.0625
Outputs:
- new_momentum: float32 [7168, 18432], P('dp', 'tensor')
- new_basis: float32 [7168, 512], P('dp')
- row_values: bfloat16 [18432, 7168], P(('tensor', 'dp'))
- row_scales: float32 [18432, 56], P(('tensor', 'dp'))
- column_values: bfloat16 [7168, 18432], P(('dp', 'tensor'))
- column_scales: float32 [7168, 144], P(('dp', 'tensor'))
The draws below stay inside these ranges and needn't reach their ends.
All inputs are finite; a program needn't handle non-finite values. Where the reference program divides by a largest or mean magnitude, that divisor is 1e-20 or more.
Results may differ from the reference program's by a relative error of at most 0.0056.
Values may be sent and summed in bfloat16 or wider, within the bound.
A program may use at most 64 MiB of HBM per device.

```python
import math
import jax
import jax.numpy as jnp
from jax import lax

D = 7168
FF = 18432
RANK = 512
TILE = 128


def shard_levels(rng, extent, split, smallest, high):
    factor_of, own = 1.0, jax.random.fold_in(rng, 6)
    for position, parts in split:
        steps = jnp.exp(jax.random.uniform(jax.random.fold_in(own, position), (parts,), jnp.float32, smallest / len(split), high / len(split)))
        factor_of = factor_of * jnp.repeat(steps, extent[position] // parts).reshape([-1 if axis == position else 1 for axis in range(len(extent))])
    return factor_of


def bell_draw(rng, extent, spread, reach, pieces=(), kind=jnp.bfloat16):
    gain = shard_levels(rng, extent, pieces, -0.22, 0.18) if pieces else 1.0
    values = jax.random.normal(rng, extent, jnp.float32) * spread * gain
    return jnp.minimum(jnp.maximum(values, -reach), reach).astype(kind)


def setup_inputs(seed: int = 0) -> dict:
    keys = jax.random.split(jax.random.key(seed), 5)
    return {
        "weight": bell_draw(keys[0], (D, FF), 0.001, 0.015625, ((0, 32), (1, 16))),
        "gradient": bell_draw(keys[1], (D, FF), 1.0, 6.0, ((0, 32), (1, 16))),
        "momentum": bell_draw(keys[2], (D, FF), 1.0, 6.0, ((0, 32), (1, 16)), jnp.float32),
        "basis": bell_draw(keys[3], (D, RANK), D ** -0.5, 0.0625, ((0, 32),), jnp.float32),
    }


decay_rate = 0.95
step_size = 0.3
epsilon = 1e-06

def quantize(block):
    rows = block.shape[0]
    width = block.shape[1]
    tiles = block.astype(jnp.float32).reshape(rows, width // TILE, TILE)
    largest = lax.optimization_barrier(jnp.max(jnp.abs(tiles), axis=2))
    values = (tiles / (largest[:, :, None] + epsilon)).astype(jnp.bfloat16)
    return (values.reshape(rows, width), largest)

def reference(weight, gradient, momentum, basis):
    highest = lax.Precision.HIGHEST
    buffer = momentum + gradient.astype(jnp.float32)
    proj = jnp.dot(buffer.T, basis, precision=highest)
    gram = jnp.dot(proj.T, proj, precision=highest)
    lower = jnp.linalg.cholesky(gram)
    ortho = jax.scipy.linalg.solve_triangular(lower, proj.T, lower=True).T
    back = jnp.dot(buffer, ortho, precision=highest)
    colsq = lax.optimization_barrier(jnp.sum(back * back, axis=0))
    new_basis = back / jnp.sqrt(colsq + epsilon)
    new_momentum = buffer - (1.0 - decay_rate) * jnp.dot(back, ortho.T, precision=highest)
    factor = step_size * math.sqrt(FF / D)
    updated = (weight.astype(jnp.float32) - factor * jnp.dot(new_basis, ortho.T, precision=highest)).astype(jnp.bfloat16)
    row_values, row_scales = quantize(updated.T)
    column_values, column_scales = quantize(updated)
    return (new_momentum, new_basis, row_values, row_scales, column_values, column_scales)
```

```python
import functools
import math

import jax
import jax.numpy as jnp
from jax import lax
from jax.experimental import pallas as pl
from jax.experimental.pallas import tpu as pltpu
from jax.sharding import PartitionSpec as P

RANK = 512
BLOCK = 128
STRIP = 8
HIGHEST = lax.Precision.HIGHEST


def dot_nt(a, b, precision=None):
    return lax.dot_general(a, b, (((1,), (1,)), ((), ())), precision=precision, preferred_element_type=jnp.float32)


def dot_nn(a, b, precision=None):
    return lax.dot_general(a, b, (((1,), (0,)), ((), ())), precision=precision, preferred_element_type=jnp.float32)


def invert_block(tiles):
    shape = (STRIP, BLOCK)
    count = BLOCK // STRIP
    row_of = lax.broadcasted_iota(jnp.int32, shape, 0)
    lane_of = lax.broadcasted_iota(jnp.int32, shape, 1)
    tiles = list(tiles)
    own = [jnp.where(lane_of == row_of + STRIP * i, 1.0, 0.0).astype(jnp.float32) for i in range(count)]
    for s in range(count):
        spread = lambda tile, m, lane: jnp.broadcast_to(tile[m:m + 1, lane:lane + 1], shape)
        small = [[spread(tiles[s], m, STRIP * s + k) for k in range(m + 1)] for m in range(STRIP)]
        rows = [jnp.broadcast_to(tiles[s][m:m + 1, :], shape) for m in range(STRIP)]
        extra = [jnp.broadcast_to(own[s][m:m + 1, :], shape) for m in range(STRIP)]
        factor = [[None] * STRIP for _ in range(STRIP)]
        inverse, root = [], []
        for k in range(STRIP):
            r = lax.rsqrt(small[k][k])
            root.append(r)
            inverse.append(r * r)
            for m in range(k + 1, STRIP):
                f = small[m][k] * inverse[k]
                factor[m][k] = f
                for j in range(k + 1, m + 1):
                    small[m][j] = small[m][j] - f * small[j][k]
                rows[m] = rows[m] - f * rows[k]
                extra[m] = extra[m] - f * extra[k]
        for i in range(s + 1, count):
            cols = [jnp.broadcast_to(tiles[i][:, STRIP * s + k:STRIP * s + k + 1], shape) for k in range(STRIP)]
            for k in range(STRIP):
                for m in range(k + 1, STRIP):
                    cols[m] = cols[m] - cols[k] * factor[m][k]
            for k in range(STRIP):
                g = cols[k] * inverse[k]
                tiles[i] = tiles[i] - g * rows[k]
                own[i] = own[i] - g * extra[k]
        done = extra[0] * root[0]
        for m in range(1, STRIP):
            done = jnp.where(row_of == m, extra[m] * root[m], done)
        own[s] = done
    return own


def cholesky_kernel(gram_ref, inv_ref, a_ref, small_ref):
    a_ref[...] = gram_ref[...]
    rank = gram_ref.shape[0]
    row_of = lax.broadcasted_iota(jnp.int32, (rank, rank), 0)
    inv_ref[...] = jnp.where(row_of == lax.broadcasted_iota(jnp.int32, (rank, rank), 1), 1.0, 0.0).astype(jnp.float32)

    def step(b, carry):
        at = pl.multiple_of(b * BLOCK, BLOCK)
        tiles = [a_ref[pl.ds(pl.multiple_of(at + STRIP * i, STRIP), STRIP), pl.ds(at, BLOCK)] for i in range(BLOCK // STRIP)]
        own = invert_block(tiles)
        for i, tile in enumerate(own):
            small_ref[pl.ds(STRIP * i, STRIP), :] = tile
        inverse = small_ref[...]
        rows = dot_nn(inverse, inv_ref[pl.ds(at, BLOCK), :], HIGHEST)
        below = lax.broadcasted_iota(jnp.int32, (rank, BLOCK), 0) >= at + BLOCK
        panel = jnp.where(below, dot_nt(a_ref[:, pl.ds(at, BLOCK)], inverse, HIGHEST), 0.0)
        inv_ref[pl.ds(at, BLOCK), :] = rows
        a_ref[...] -= dot_nt(panel, panel, HIGHEST)
        inv_ref[...] -= dot_nn(panel, rows, HIGHEST)
        return carry

    lax.fori_loop(0, rank // BLOCK, step, 0)


def inverse_factor(gram):
    return pl.pallas_call(
        cholesky_kernel,
        out_shape=jax.ShapeDtypeStruct(gram.shape, jnp.float32),
        in_specs=[pl.BlockSpec(memory_space=pltpu.VMEM)],
        out_specs=pl.BlockSpec(memory_space=pltpu.VMEM),
        scratch_shapes=[pltpu.VMEM(gram.shape, jnp.float32), pltpu.VMEM((BLOCK, BLOCK), jnp.float32)],
        compiler_params=pltpu.CompilerParams(vmem_limit_bytes=48 << 20),
    )(gram)


D = 7168
FF = 18432
TILE = 128
decay_rate = 0.95
step_size = 0.3
epsilon = 1e-06

DP = 32
TENSOR = 16
CHIPS = 16
SLAB = RANK // DP
MESH = pl.DeviceIdType.MESH
VMEM = pl.BlockSpec(memory_space=pltpu.VMEM)


def halves(x):
    high = x.astype(jnp.bfloat16)
    return high, (x - high.astype(jnp.float32)).astype(jnp.bfloat16)


def remote(src, dst, send, recv, dp, tensor):
    return pltpu.make_async_remote_copy(
        src_ref=src, dst_ref=dst, send_sem=send, recv_sem=recv, device_id=(dp, tensor), device_id_type=MESH
    )


def slab_rows(dp):
    return pl.ds(pl.multiple_of(SLAB * (CHIPS * lax.rem(dp, 2) + dp // 2), SLAB), SLAB)


def spread_slabs(buffer, dp, tensor, send, recv, pass_send, pass_recv):
    core, chip = lax.rem(dp, 2), dp // 2
    other = dp + 1 - 2 * core

    def rows(which):
        return buffer.at[slab_rows(which), :]

    def copy(step):
        to = lax.rem(chip + step, CHIPS)
        return remote(rows(dp), rows(dp), send.at[step], recv.at[chip], 2 * to + core, tensor)

    def arrival(source):
        return remote(rows(2 * source + core), rows(2 * source + core), send.at[0], recv.at[source], dp, tensor)

    def onward(source):
        return remote(rows(2 * source + core), rows(2 * source + core), pass_send.at[source], pass_recv.at[source], other, tensor)

    def passed(source):
        there = rows(2 * source + 1 - core)
        return remote(there, there, pass_send.at[source], pass_recv.at[source], other, tensor)

    def begin(step, carry):
        copy(step).start()
        return carry

    def forward(step, carry):
        source = lax.rem(chip + CHIPS - step, CHIPS)
        arrival(source).wait_recv()
        onward(source).start()
        return carry

    def finish(step, carry):
        passed(lax.rem(chip + CHIPS - step, CHIPS)).wait_recv()
        return carry

    def drain(step, carry):
        copy(step).wait_send()
        return carry

    def drain_pass(step, carry):
        onward(lax.rem(chip + CHIPS - step, CHIPS)).wait_send()
        return carry

    lax.fori_loop(1, CHIPS, begin, 0)
    onward(chip).start()
    lax.fori_loop(1, CHIPS, forward, 0)
    lax.fori_loop(0, CHIPS, finish, 0)
    lax.fori_loop(1, CHIPS, drain, 0)
    lax.fori_loop(0, CHIPS, drain_pass, 0)


def greet_dp(barrier, dp, tensor):
    core, chip = lax.rem(dp, 2), dp // 2

    def greet(step, carry):
        to = lax.rem(chip + step, CHIPS)
        pl.semaphore_signal(barrier, inc=1, device_id=(2 * to + core, tensor), device_id_type=MESH)
        return carry

    lax.fori_loop(1, CHIPS, greet, 0)
    pl.semaphore_signal(barrier, inc=1, device_id=(dp + 1 - 2 * core, tensor), device_id_type=MESH)


def proj_kernel(momentum, gradient, basis, proj, high, low, basis_high, basis_low, pair_out, pair_in, part, inbox,
                pair_sems, send, recv, all_send, all_recv, pass_send, pass_recv):
    dp, tensor = lax.axis_index("dp"), lax.axis_index("tensor")
    core, chip = lax.rem(dp, 2), dp // 2
    other = dp + 1 - 2 * core
    half = RANK // 2

    barrier = pltpu.get_barrier_semaphore()
    greet_dp(barrier, dp, tensor)

    columns = momentum.shape[1]
    width = columns // 3
    for j in range(3):
        span = pl.ds(j * width, width)
        high[:, span], low[:, span] = halves(momentum[:, span] + gradient[:, span].astype(jnp.float32))
    basis_high[...], basis_low[...] = halves(jnp.transpose(basis[...]))

    def product(first, j):
        span = pl.ds(j * width, width)
        rows = pl.ds(pl.multiple_of(first, half), half)
        return (
            dot_nn(basis_high[rows, :], high[:, span])
            + dot_nn(basis_high[rows, :], low[:, span])
            + dot_nn(basis_low[rows, :], high[:, span])
        )

    for j in range(3):
        pair_out[:, pl.ds(j * width, width)] = product((1 - core) * half, j)
    pl.semaphore_wait(barrier, CHIPS)
    swap = remote(pair_out, pair_in, pair_sems.at[0], pair_sems.at[1], other, tensor)
    swap.start()
    mine = [product(core * half, j) for j in range(3)]
    swap.wait_recv()
    for j in range(3):
        span = pl.ds(j * width, width)
        part[:, span] = (mine[j] + pair_in[:, span]).astype(jnp.bfloat16)

    def slab(which):
        return part.at[pl.ds(pl.multiple_of(which * SLAB, SLAB), SLAB), :]

    def copy(step):
        to = lax.rem(chip + step, CHIPS)
        return remote(slab(to), inbox.at[chip], send.at[step], recv.at[chip], 2 * to + core, tensor)

    def begin(step, carry):
        copy(step).start()
        return carry

    def arrive(step, total):
        source = lax.rem(chip + CHIPS - step, CHIPS)
        remote(inbox.at[source], inbox.at[source], send.at[0], recv.at[source], other, tensor).wait_recv()
        return total + inbox[source].astype(jnp.float32)

    def drain(step, carry):
        copy(step).wait_send()
        return carry

    lax.fori_loop(1, CHIPS, begin, 0)
    total = part[pl.ds(pl.multiple_of(chip * SLAB, SLAB), SLAB), :].astype(jnp.float32)
    total = lax.fori_loop(1, CHIPS, arrive, total)
    proj[slab_rows(dp), :] = total.astype(jnp.bfloat16)
    spread_slabs(proj, dp, tensor, all_send, all_recv, pass_send, pass_recv)
    lax.fori_loop(1, CHIPS, drain, 0)
    swap.wait_send()


def proj_transposed(momentum, gradient, basis):
    rows, columns = momentum.shape
    half = RANK // 2
    dma = pltpu.SemaphoreType.DMA
    return pl.pallas_call(
        proj_kernel,
        out_shape=jax.ShapeDtypeStruct((RANK, columns), jnp.bfloat16),
        in_specs=[VMEM] * 3,
        out_specs=VMEM,
        scratch_shapes=[
            pltpu.VMEM((rows, columns), jnp.bfloat16),
            pltpu.VMEM((rows, columns), jnp.bfloat16),
            pltpu.VMEM((RANK, rows), jnp.bfloat16),
            pltpu.VMEM((RANK, rows), jnp.bfloat16),
            pltpu.VMEM((half, columns), jnp.float32),
            pltpu.VMEM((half, columns), jnp.float32),
            pltpu.VMEM((half, columns), jnp.bfloat16),
            pltpu.VMEM((CHIPS, SLAB, columns), jnp.bfloat16),
            dma((2,)), dma((CHIPS,)), dma((CHIPS,)), dma((CHIPS,)), dma((CHIPS,)), dma((CHIPS,)), dma((CHIPS,)),
        ],
        compiler_params=pltpu.CompilerParams(collective_id=0, has_side_effects=True, vmem_limit_bytes=48 << 20),
    )(momentum, gradient, basis)


OWNERS = 8
WIDE_ROWS, WIDE_COLUMNS = 64, 128


def sums_kernel(momentum, gradient, proj, gram, wide, gram_part, gram_inbox, wide_part, wide_inbox, wide_all,
                tile_send, tile_recv, back_send, back_recv, wide_send, wide_recv, out_send, out_recv,
                all_send, all_recv, pass_send, pass_recv):
    dp, tensor = lax.axis_index("dp"), lax.axis_index("tensor")
    rows = momentum.shape[0]
    barrier = pltpu.get_barrier_semaphore()
    greet_dp(barrier, dp, tensor)

    def greet(step, carry):
        to = lax.rem(tensor + step, TENSOR)
        pl.semaphore_signal(barrier, inc=1, device_id=(dp, to), device_id_type=MESH)
        return carry

    lax.fori_loop(1, TENSOR, greet, 0)

    gram_part[...] = dot_nt(proj[slab_rows(dp), :], proj[...])
    pl.semaphore_wait(barrier, CHIPS + TENSOR - 1)

    def tile(ref, first, owner):
        return ref.at[
            pl.ds(pl.multiple_of(first + 8 * (owner // 4), 8), 8), pl.ds(pl.multiple_of(128 * lax.rem(owner, 4), 128), 128)
        ]

    def tile_copy(owner):
        return remote(tile(gram_part, 0, owner), gram_inbox.at[tensor], tile_send.at[owner], tile_recv.at[tensor], dp, owner)

    def tile_begin(owner, carry):
        @pl.when(owner != tensor)
        def _():
            tile_copy(owner).start()

        return carry

    lax.fori_loop(0, OWNERS, tile_begin, 0)

    high, low = halves(momentum[...] + gradient[...].astype(jnp.float32))
    wide_part[:rows, :] = (dot_nt(high, proj[...]) + dot_nt(low, proj[...])).astype(jnp.bfloat16)
    wide_part[rows:, :] = jnp.zeros((wide_part.shape[0] - rows, RANK), jnp.bfloat16)

    def piece(ref, which):
        return ref.at[
            pl.ds(pl.multiple_of(WIDE_ROWS * (which // 4), WIDE_ROWS), WIDE_ROWS),
            pl.ds(pl.multiple_of(WIDE_COLUMNS * lax.rem(which, 4), WIDE_COLUMNS), WIDE_COLUMNS),
        ]

    def wide_copy(step):
        to = lax.rem(tensor + step, TENSOR)
        return remote(piece(wide_part, to), wide_inbox.at[tensor], wide_send.at[step], wide_recv.at[tensor], dp, to)

    def wide_begin(step, carry):
        wide_copy(step).start()
        return carry

    lax.fori_loop(1, TENSOR, wide_begin, 0)

    first = SLAB * (CHIPS * lax.rem(dp, 2) + dp // 2)

    def back_copy(step):
        to = lax.rem(tensor + step, TENSOR)
        here = tile(gram, first, tensor)
        return remote(here, here, back_send.at[step], back_recv.at[tensor], dp, to)

    @pl.when(tensor < OWNERS)
    def _():
        def arrive(step, total):
            source = lax.rem(tensor + step, TENSOR)
            there = gram_inbox.at[source]
            remote(there, there, tile_send.at[0], tile_recv.at[source], dp, tensor).wait_recv()
            return total + gram_inbox[source]

        def back_begin(step, carry):
            back_copy(step).start()
            return carry

        total = lax.fori_loop(1, TENSOR, arrive, tile(gram_part, 0, tensor)[...])
        tile(gram, first, tensor)[...] = total
        lax.fori_loop(1, TENSOR, back_begin, 0)

    def wide_arrive(step, total):
        source = lax.rem(tensor + step, TENSOR)
        there = wide_inbox.at[source]
        remote(there, there, wide_send.at[0], wide_recv.at[source], dp, tensor).wait_recv()
        return total + wide_inbox[source].astype(jnp.float32)

    def out_copy(step):
        to = lax.rem(tensor + step, TENSOR)
        here = piece(wide_all, tensor)
        return remote(here, here, out_send.at[step], out_recv.at[tensor], dp, to)

    def out_begin(step, carry):
        out_copy(step).start()
        return carry

    def back_arrive(owner, carry):
        @pl.when(owner != tensor)
        def _():
            there = tile(gram, first, owner)
            remote(there, there, back_send.at[0], back_recv.at[owner], dp, tensor).wait_recv()

        return carry

    lax.fori_loop(0, OWNERS, back_arrive, 0)
    spread_slabs(gram, dp, tensor, all_send, all_recv, pass_send, pass_recv)

    piece(wide_all, tensor)[...] = lax.fori_loop(
        1, TENSOR, wide_arrive, piece(wide_part, tensor)[...].astype(jnp.float32)
    )
    lax.fori_loop(1, TENSOR, out_begin, 0)

    def out_arrive(step, carry):
        source = lax.rem(tensor + step, TENSOR)
        there = piece(wide_all, source)
        remote(there, there, out_send.at[0], out_recv.at[source], dp, tensor).wait_recv()
        return carry

    lax.fori_loop(1, TENSOR, out_arrive, 0)
    wide[...] = wide_all[:rows, :]

    def tile_drain(owner, carry):
        @pl.when(owner != tensor)
        def _():
            tile_copy(owner).wait_send()

        return carry

    def drain(step, carry):
        wide_copy(step).wait_send()
        out_copy(step).wait_send()

        @pl.when(tensor < OWNERS)
        def _():
            back_copy(step).wait_send()

        return carry

    lax.fori_loop(0, OWNERS, tile_drain, 0)
    lax.fori_loop(1, TENSOR, drain, 0)


def gram_and_wide(momentum, gradient, proj):
    rows = momentum.shape[0]
    padded = TENSOR // 4 * WIDE_ROWS
    dma = pltpu.SemaphoreType.DMA
    return pl.pallas_call(
        sums_kernel,
        out_shape=(jax.ShapeDtypeStruct((RANK, RANK), jnp.float32), jax.ShapeDtypeStruct((rows, RANK), jnp.float32)),
        in_specs=[VMEM] * 3,
        out_specs=(VMEM, VMEM),
        scratch_shapes=[
            pltpu.VMEM((SLAB, RANK), jnp.float32),
            pltpu.VMEM((TENSOR, 8, 128), jnp.float32),
            pltpu.VMEM((padded, RANK), jnp.bfloat16),
            pltpu.VMEM((TENSOR, WIDE_ROWS, WIDE_COLUMNS), jnp.bfloat16),
            pltpu.VMEM((padded, RANK), jnp.float32),
            dma((OWNERS,)), dma((TENSOR,)), dma((TENSOR,)), dma((OWNERS,)),
            dma((TENSOR,)), dma((TENSOR,)), dma((TENSOR,)), dma((TENSOR,)),
            dma((CHIPS,)), dma((CHIPS,)), dma((CHIPS,)), dma((CHIPS,)),
        ],
        compiler_params=pltpu.CompilerParams(collective_id=1, has_side_effects=True, vmem_limit_bytes=48 << 20),
    )(momentum, gradient, proj)


def basis_kernel(wide, inverse, back, new_basis, inbox, send, recv):
    dp, tensor = lax.axis_index("dp"), lax.axis_index("tensor")
    barrier = pltpu.get_barrier_semaphore()

    def greet(step, carry):
        pl.semaphore_signal(barrier, inc=1, device_id=(lax.rem(dp + step, DP), tensor), device_id_type=MESH)
        return carry

    lax.fori_loop(1, DP, greet, 0)
    own = dot_nt(wide[...], inverse[...], HIGHEST)
    back[...] = own
    inbox[dp] = jnp.sum((own * own).reshape(own.shape[0] // 8, 8, own.shape[1]), axis=0)
    pl.semaphore_wait(barrier, DP - 1)

    def copy(step):
        return remote(inbox.at[dp], inbox.at[dp], send.at[step], recv.at[dp], lax.rem(dp + step, DP), tensor)

    def begin(step, carry):
        copy(step).start()
        return carry

    def arrive(step, carry):
        there = inbox.at[lax.rem(dp + step, DP)]
        remote(there, there, send.at[0], recv.at[lax.rem(dp + step, DP)], dp, tensor).wait_recv()
        return carry

    def drain(step, carry):
        copy(step).wait_send()
        return carry

    lax.fori_loop(1, DP, begin, 0)
    lax.fori_loop(1, DP, arrive, 0)
    total = inbox[0]
    for source in range(1, DP):
        total += inbox[source]
    colsq = jnp.sum(total, axis=0, keepdims=True)
    new_basis[...] = own / jnp.sqrt(colsq + epsilon)
    lax.fori_loop(1, DP, drain, 0)


def back_and_basis(wide, inverse):
    dma = pltpu.SemaphoreType.DMA
    return pl.pallas_call(
        basis_kernel,
        out_shape=(jax.ShapeDtypeStruct(wide.shape, jnp.float32),) * 2,
        in_specs=[VMEM] * 2,
        out_specs=(VMEM, VMEM),
        scratch_shapes=[pltpu.VMEM((DP, 8, RANK), jnp.float32), dma((DP,)), dma((DP,))],
        compiler_params=pltpu.CompilerParams(collective_id=2, has_side_effects=True, vmem_limit_bytes=48 << 20),
    )(wide, inverse)


def quantize(block):
    rows = block.shape[0]
    width = block.shape[1]
    tiles = block.astype(jnp.float32).reshape(rows, width // TILE, TILE)
    largest = jnp.max(jnp.abs(tiles), axis=2)
    values = (tiles / (largest[:, :, None] + epsilon)).astype(jnp.bfloat16)
    return (values.reshape(rows, width), largest)


def on_device(weight, gradient, momentum, basis):
    high = lax.Precision.HIGH
    proj = proj_transposed(momentum, gradient, basis)
    gram, wide = gram_and_wide(momentum, gradient, proj)
    inverse = inverse_factor(gram)
    back, new_basis = back_and_basis(wide, inverse)
    inverse_high, inverse_low = halves(inverse)
    ortho = dot_nn(inverse_high, proj) + dot_nn(inverse_low, proj)
    buffer = momentum + gradient.astype(jnp.float32)
    new_momentum = buffer - (1.0 - decay_rate) * jnp.dot(back, ortho, precision=high)
    factor = step_size * math.sqrt(FF / D)
    updated = (weight.astype(jnp.float32) - factor * jnp.dot(new_basis, ortho, precision=high)).astype(jnp.bfloat16)
    full_rows = lax.all_to_all(updated.T, "dp", split_axis=0, concat_axis=1, tiled=True)
    row_values, row_scales = quantize(full_rows)
    full_columns = lax.all_to_all(updated, "tensor", split_axis=0, concat_axis=1, tiled=True)
    column_values, column_scales = quantize(full_columns)
    return (new_momentum, new_basis, row_values, row_scales, column_values, column_scales)


def solution(mesh):
    placed = (P("dp", "tensor"), P("dp", "tensor"), P("dp", "tensor"), P("dp", None))
    return jax.shard_map(
        on_device,
        mesh=mesh,
        in_specs=placed,
        out_specs=(
            P("dp", "tensor"),
            P("dp", None),
            P(("tensor", "dp"), None),
            P(("tensor", "dp"), None),
            P(("dp", "tensor"), None),
            P(("dp", "tensor"), None),
        ),
        check_vma=False,
    )
```

```python
import functools
import math

import jax
import jax.numpy as jnp
from jax import lax
from jax.experimental import pallas as pl
from jax.experimental.pallas import tpu as pltpu
from jax.sharding import PartitionSpec as P

RANK = 512
BLOCK = 128
STRIP = 8
HIGHEST = lax.Precision.HIGHEST


def dot_nt(a, b, precision=None):
    return lax.dot_general(a, b, (((1,), (1,)), ((), ())), precision=precision, preferred_element_type=jnp.float32)


def dot_nn(a, b, precision=None):
    return lax.dot_general(a, b, (((1,), (0,)), ((), ())), precision=precision, preferred_element_type=jnp.float32)


def invert_block(tiles):
    shape = (STRIP, BLOCK)
    count = BLOCK // STRIP
    row_of = lax.broadcasted_iota(jnp.int32, shape, 0)
    lane_of = lax.broadcasted_iota(jnp.int32, shape, 1)
    tiles = list(tiles)
    own = [jnp.where(lane_of == row_of + STRIP * i, 1.0, 0.0).astype(jnp.float32) for i in range(count)]
    for s in range(count):
        spread = lambda tile, m, lane: jnp.broadcast_to(tile[m:m + 1, lane:lane + 1], shape)
        small = [[spread(tiles[s], m, STRIP * s + k) for k in range(m + 1)] for m in range(STRIP)]
        rows = [jnp.broadcast_to(tiles[s][m:m + 1, :], shape) for m in range(STRIP)]
        extra = [jnp.broadcast_to(own[s][m:m + 1, :], shape) for m in range(STRIP)]
        factor = [[None] * STRIP for _ in range(STRIP)]
        inverse, root = [], []
        for k in range(STRIP):
            r = lax.rsqrt(small[k][k])
            root.append(r)
            inverse.append(r * r)
            for m in range(k + 1, STRIP):
                f = small[m][k] * inverse[k]
                factor[m][k] = f
                for j in range(k + 1, m + 1):
                    small[m][j] = small[m][j] - f * small[j][k]
                rows[m] = rows[m] - f * rows[k]
                extra[m] = extra[m] - f * extra[k]
        for i in range(s + 1, count):
            cols = [jnp.broadcast_to(tiles[i][:, STRIP * s + k:STRIP * s + k + 1], shape) for k in range(STRIP)]
            for k in range(STRIP):
                for m in range(k + 1, STRIP):
                    cols[m] = cols[m] - cols[k] * factor[m][k]
            for k in range(STRIP):
                g = cols[k] * inverse[k]
                tiles[i] = tiles[i] - g * rows[k]
                own[i] = own[i] - g * extra[k]
        done = extra[0] * root[0]
        for m in range(1, STRIP):
            done = jnp.where(row_of == m, extra[m] * root[m], done)
        own[s] = done
    return own


def cholesky_kernel(gram_ref, inv_ref, a_ref, small_ref):
    a_ref[...] = gram_ref[...]
    rank = gram_ref.shape[0]
    row_of = lax.broadcasted_iota(jnp.int32, (rank, rank), 0)
    inv_ref[...] = jnp.where(row_of == lax.broadcasted_iota(jnp.int32, (rank, rank), 1), 1.0, 0.0).astype(jnp.float32)

    def step(b, carry):
        at = pl.multiple_of(b * BLOCK, BLOCK)
        tiles = [a_ref[pl.ds(pl.multiple_of(at + STRIP * i, STRIP), STRIP), pl.ds(at, BLOCK)] for i in range(BLOCK // STRIP)]
        own = invert_block(tiles)
        for i, tile in enumerate(own):
            small_ref[pl.ds(STRIP * i, STRIP), :] = tile
        inverse = small_ref[...]
        rows = dot_nn(inverse, inv_ref[pl.ds(at, BLOCK), :], HIGHEST)
        below = lax.broadcasted_iota(jnp.int32, (rank, BLOCK), 0) >= at + BLOCK
        panel = jnp.where(below, dot_nt(a_ref[:, pl.ds(at, BLOCK)], inverse, HIGHEST), 0.0)
        inv_ref[pl.ds(at, BLOCK), :] = rows
        a_ref[...] -= dot_nt(panel, panel, HIGHEST)
        inv_ref[...] -= dot_nn(panel, rows, HIGHEST)
        return carry

    lax.fori_loop(0, rank // BLOCK, step, 0)


def inverse_factor(gram):
    return pl.pallas_call(
        cholesky_kernel,
        out_shape=jax.ShapeDtypeStruct(gram.shape, jnp.float32),
        in_specs=[pl.BlockSpec(memory_space=pltpu.VMEM)],
        out_specs=pl.BlockSpec(memory_space=pltpu.VMEM),
        scratch_shapes=[pltpu.VMEM(gram.shape, jnp.float32), pltpu.VMEM((BLOCK, BLOCK), jnp.float32)],
        compiler_params=pltpu.CompilerParams(vmem_limit_bytes=48 << 20),
    )(gram)


D = 7168
FF = 18432
TILE = 128
decay_rate = 0.95
step_size = 0.3
epsilon = 1e-06

DP = 32
TENSOR = 16
CHIPS = 16
SLAB = RANK // DP
MESH = pl.DeviceIdType.MESH
VMEM = pl.BlockSpec(memory_space=pltpu.VMEM)


def halves(x):
    high = x.astype(jnp.bfloat16)
    return high, (x - high.astype(jnp.float32)).astype(jnp.bfloat16)


def remote(src, dst, send, recv, dp, tensor):
    return pltpu.make_async_remote_copy(
        src_ref=src, dst_ref=dst, send_sem=send, recv_sem=recv, device_id=(dp, tensor), device_id_type=MESH
    )


def slab_rows(dp):
    return pl.ds(pl.multiple_of(SLAB * (CHIPS * lax.rem(dp, 2) + dp // 2), SLAB), SLAB)


def spread_slabs(buffer, dp, tensor, send, recv, pass_send, pass_recv):
    core, chip = lax.rem(dp, 2), dp // 2
    other = dp + 1 - 2 * core

    def rows(which):
        return buffer.at[slab_rows(which), :]

    def copy(step):
        to = lax.rem(chip + step, CHIPS)
        return remote(rows(dp), rows(dp), send.at[step], recv.at[chip], 2 * to + core, tensor)

    def arrival(source):
        return remote(rows(2 * source + core), rows(2 * source + core), send.at[0], recv.at[source], dp, tensor)

    def onward(source):
        return remote(rows(2 * source + core), rows(2 * source + core), pass_send.at[source], pass_recv.at[source], other, tensor)

    def passed(source):
        there = rows(2 * source + 1 - core)
        return remote(there, there, pass_send.at[source], pass_recv.at[source], other, tensor)

    def begin(step, carry):
        copy(step).start()
        return carry

    def forward(step, carry):
        source = lax.rem(chip + CHIPS - step, CHIPS)
        arrival(source).wait_recv()
        onward(source).start()
        return carry

    def finish(step, carry):
        passed(lax.rem(chip + CHIPS - step, CHIPS)).wait_recv()
        return carry

    def drain(step, carry):
        copy(step).wait_send()
        return carry

    def drain_pass(step, carry):
        onward(lax.rem(chip + CHIPS - step, CHIPS)).wait_send()
        return carry

    lax.fori_loop(1, CHIPS, begin, 0)
    onward(chip).start()
    lax.fori_loop(1, CHIPS, forward, 0)
    lax.fori_loop(0, CHIPS, finish, 0)
    lax.fori_loop(1, CHIPS, drain, 0)
    lax.fori_loop(0, CHIPS, drain_pass, 0)


def greet_dp(barrier, dp, tensor):
    core, chip = lax.rem(dp, 2), dp // 2

    def greet(step, carry):
        to = lax.rem(chip + step, CHIPS)
        pl.semaphore_signal(barrier, inc=1, device_id=(2 * to + core, tensor), device_id_type=MESH)
        return carry

    lax.fori_loop(1, CHIPS, greet, 0)
    pl.semaphore_signal(barrier, inc=1, device_id=(dp + 1 - 2 * core, tensor), device_id_type=MESH)


def proj_kernel(momentum, gradient, basis, proj, high, low, basis_high, basis_low, pair_out, pair_in, part, inbox,
                pair_sems, send, recv, all_send, all_recv, pass_send, pass_recv):
    dp, tensor = lax.axis_index("dp"), lax.axis_index("tensor")
    core, chip = lax.rem(dp, 2), dp // 2
    other = dp + 1 - 2 * core
    half = RANK // 2

    barrier = pltpu.get_barrier_semaphore()
    greet_dp(barrier, dp, tensor)

    columns = momentum.shape[1]
    width = columns // 3
    for j in range(3):
        span = pl.ds(j * width, width)
        high[:, span], low[:, span] = halves(momentum[:, span] + gradient[:, span].astype(jnp.float32))
    basis_high[...], basis_low[...] = halves(jnp.transpose(basis[...]))

    def product(first, j):
        span = pl.ds(j * width, width)
        rows = pl.ds(pl.multiple_of(first, half), half)
        return (
            dot_nn(basis_high[rows, :], high[:, span])
            + dot_nn(basis_high[rows, :], low[:, span])
            + dot_nn(basis_low[rows, :], high[:, span])
        )

    for j in range(3):
        pair_out[:, pl.ds(j * width, width)] = product((1 - core) * half, j)
    pl.semaphore_wait(barrier, CHIPS)
    swap = remote(pair_out, pair_in, pair_sems.at[0], pair_sems.at[1], other, tensor)
    swap.start()
    mine = [product(core * half, j) for j in range(3)]
    swap.wait_recv()
    for j in range(3):
        span = pl.ds(j * width, width)
        part[:, span] = (mine[j] + pair_in[:, span]).astype(jnp.bfloat16)

    def slab(which):
        return part.at[pl.ds(pl.multiple_of(which * SLAB, SLAB), SLAB), :]

    def copy(step):
        to = lax.rem(chip + step, CHIPS)
        return remote(slab(to), inbox.at[chip], send.at[step], recv.at[chip], 2 * to + core, tensor)

    def begin(step, carry):
        copy(step).start()
        return carry

    def arrive(step, total):
        source = lax.rem(chip + CHIPS - step, CHIPS)
        remote(inbox.at[source], inbox.at[source], send.at[0], recv.at[source], other, tensor).wait_recv()
        return total + inbox[source].astype(jnp.float32)

    def drain(step, carry):
        copy(step).wait_send()
        return carry

    lax.fori_loop(1, CHIPS, begin, 0)
    total = part[pl.ds(pl.multiple_of(chip * SLAB, SLAB), SLAB), :].astype(jnp.float32)
    total = lax.fori_loop(1, CHIPS, arrive, total)
    proj[slab_rows(dp), :] = total.astype(jnp.bfloat16)
    spread_slabs(proj, dp, tensor, all_send, all_recv, pass_send, pass_recv)
    lax.fori_loop(1, CHIPS, drain, 0)
    swap.wait_send()


def proj_transposed(momentum, gradient, basis):
    rows, columns = momentum.shape
    half = RANK // 2
    dma = pltpu.SemaphoreType.DMA
    return pl.pallas_call(
        proj_kernel,
        out_shape=jax.ShapeDtypeStruct((RANK, columns), jnp.bfloat16),
        in_specs=[VMEM] * 3,
        out_specs=VMEM,
        scratch_shapes=[
            pltpu.VMEM((rows, columns), jnp.bfloat16),
            pltpu.VMEM((rows, columns), jnp.bfloat16),
            pltpu.VMEM((RANK, rows), jnp.bfloat16),
            pltpu.VMEM((RANK, rows), jnp.bfloat16),
            pltpu.VMEM((half, columns), jnp.float32),
            pltpu.VMEM((half, columns), jnp.float32),
            pltpu.VMEM((half, columns), jnp.bfloat16),
            pltpu.VMEM((CHIPS, SLAB, columns), jnp.bfloat16),
            dma((2,)), dma((CHIPS,)), dma((CHIPS,)), dma((CHIPS,)), dma((CHIPS,)), dma((CHIPS,)), dma((CHIPS,)),
        ],
        compiler_params=pltpu.CompilerParams(collective_id=0, has_side_effects=True, vmem_limit_bytes=48 << 20),
    )(momentum, gradient, basis)


OWNERS = 8
WIDE_ROWS, WIDE_COLUMNS = 64, 128


def sums_kernel(momentum, gradient, proj, gram, wide, gram_part, gram_inbox, wide_part, wide_inbox, wide_all,
                tile_send, tile_recv, back_send, back_recv, wide_send, wide_recv, out_send, out_recv,
                all_send, all_recv, pass_send, pass_recv):
    dp, tensor = lax.axis_index("dp"), lax.axis_index("tensor")
    rows = momentum.shape[0]
    barrier = pltpu.get_barrier_semaphore()
    greet_dp(barrier, dp, tensor)

    def greet(step, carry):
        to = lax.rem(tensor + step, TENSOR)
        pl.semaphore_signal(barrier, inc=1, device_id=(dp, to), device_id_type=MESH)
        return carry

    lax.fori_loop(1, TENSOR, greet, 0)

    gram_part[...] = dot_nt(proj[slab_rows(dp), :], proj[...])
    pl.semaphore_wait(barrier, CHIPS + TENSOR - 1)

    def tile(ref, first, owner):
        return ref.at[
            pl.ds(pl.multiple_of(first + 8 * (owner // 4), 8), 8), pl.ds(pl.multiple_of(128 * lax.rem(owner, 4), 128), 128)
        ]

    def tile_copy(owner):
        return remote(tile(gram_part, 0, owner), gram_inbox.at[tensor], tile_send.at[owner], tile_recv.at[tensor], dp, owner)

    def tile_begin(owner, carry):
        @pl.when(owner != tensor)
        def _():
            tile_copy(owner).start()

        return carry

    lax.fori_loop(0, OWNERS, tile_begin, 0)

    high, low = halves(momentum[...] + gradient[...].astype(jnp.float32))
    wide_part[:rows, :] = (dot_nt(high, proj[...]) + dot_nt(low, proj[...])).astype(jnp.bfloat16)
    wide_part[rows:, :] = jnp.zeros((wide_part.shape[0] - rows, RANK), jnp.bfloat16)

    def piece(ref, which):
        return ref.at[
            pl.ds(pl.multiple_of(WIDE_ROWS * (which // 4), WIDE_ROWS), WIDE_ROWS),
            pl.ds(pl.multiple_of(WIDE_COLUMNS * lax.rem(which, 4), WIDE_COLUMNS), WIDE_COLUMNS),
        ]

    def wide_copy(step):
        to = lax.rem(tensor + step, TENSOR)
        return remote(piece(wide_part, to), wide_inbox.at[tensor], wide_send.at[step], wide_recv.at[tensor], dp, to)

    def wide_begin(step, carry):
        wide_copy(step).start()
        return carry

    lax.fori_loop(1, TENSOR, wide_begin, 0)

    first = SLAB * (CHIPS * lax.rem(dp, 2) + dp // 2)

    def back_copy(step):
        to = lax.rem(tensor + step, TENSOR)
        here = tile(gram, first, tensor)
        return remote(here, here, back_send.at[step], back_recv.at[tensor], dp, to)

    @pl.when(tensor < OWNERS)
    def _():
        def arrive(step, total):
            source = lax.rem(tensor + step, TENSOR)
            there = gram_inbox.at[source]
            remote(there, there, tile_send.at[0], tile_recv.at[source], dp, tensor).wait_recv()
            return total + gram_inbox[source]

        def back_begin(step, carry):
            back_copy(step).start()
            return carry

        total = lax.fori_loop(1, TENSOR, arrive, tile(gram_part, 0, tensor)[...])
        tile(gram, first, tensor)[...] = total
        lax.fori_loop(1, TENSOR, back_begin, 0)

    def wide_arrive(step, total):
        source = lax.rem(tensor + step, TENSOR)
        there = wide_inbox.at[source]
        remote(there, there, wide_send.at[0], wide_recv.at[source], dp, tensor).wait_recv()
        return total + wide_inbox[source].astype(jnp.float32)

    def out_copy(step):
        to = lax.rem(tensor + step, TENSOR)
        here = piece(wide_all, tensor)
        return remote(here, here, out_send.at[step], out_recv.at[tensor], dp, to)

    def out_begin(step, carry):
        out_copy(step).start()
        return carry

    def back_arrive(owner, carry):
        @pl.when(owner != tensor)
        def _():
            there = tile(gram, first, owner)
            remote(there, there, back_send.at[0], back_recv.at[owner], dp, tensor).wait_recv()

        return carry

    lax.fori_loop(0, OWNERS, back_arrive, 0)
    spread_slabs(gram, dp, tensor, all_send, all_recv, pass_send, pass_recv)

    piece(wide_all, tensor)[...] = lax.fori_loop(
        1, TENSOR, wide_arrive, piece(wide_part, tensor)[...].astype(jnp.float32)
    )
    lax.fori_loop(1, TENSOR, out_begin, 0)

    def out_arrive(step, carry):
        source = lax.rem(tensor + step, TENSOR)
        there = piece(wide_all, source)
        remote(there, there, out_send.at[0], out_recv.at[source], dp, tensor).wait_recv()
        return carry

    lax.fori_loop(1, TENSOR, out_arrive, 0)
    wide[...] = wide_all[:rows, :]

    def tile_drain(owner, carry):
        @pl.when(owner != tensor)
        def _():
            tile_copy(owner).wait_send()

        return carry

    def drain(step, carry):
        wide_copy(step).wait_send()
        out_copy(step).wait_send()

        @pl.when(tensor < OWNERS)
        def _():
            back_copy(step).wait_send()

        return carry

    lax.fori_loop(0, OWNERS, tile_drain, 0)
    lax.fori_loop(1, TENSOR, drain, 0)


def gram_and_wide(momentum, gradient, proj):
    rows = momentum.shape[0]
    padded = TENSOR // 4 * WIDE_ROWS
    dma = pltpu.SemaphoreType.DMA
    return pl.pallas_call(
        sums_kernel,
        out_shape=(jax.ShapeDtypeStruct((RANK, RANK), jnp.float32), jax.ShapeDtypeStruct((rows, RANK), jnp.float32)),
        in_specs=[VMEM] * 3,
        out_specs=(VMEM, VMEM),
        scratch_shapes=[
            pltpu.VMEM((SLAB, RANK), jnp.float32),
            pltpu.VMEM((TENSOR, 8, 128), jnp.float32),
            pltpu.VMEM((padded, RANK), jnp.bfloat16),
            pltpu.VMEM((TENSOR, WIDE_ROWS, WIDE_COLUMNS), jnp.bfloat16),
            pltpu.VMEM((padded, RANK), jnp.float32),
            dma((OWNERS,)), dma((TENSOR,)), dma((TENSOR,)), dma((OWNERS,)),
            dma((TENSOR,)), dma((TENSOR,)), dma((TENSOR,)), dma((TENSOR,)),
            dma((CHIPS,)), dma((CHIPS,)), dma((CHIPS,)), dma((CHIPS,)),
        ],
        compiler_params=pltpu.CompilerParams(collective_id=1, has_side_effects=True, vmem_limit_bytes=48 << 20),
    )(momentum, gradient, proj)


CHUNK = 48
ROWS_OUT = FF // TENSOR // DP
COLUMNS_OUT = D // DP // TENSOR
TURN = 32


def apply_kernel(weight, momentum, gradient, wide, inverse, proj,
                 new_momentum, new_basis, row_values, row_scales, column_values, column_scales,
                 back_high, basis_high, basis_low, ortho_high, ortho_low, square_inbox, update, turned, flipped, row_out, row_in, column_out, column_in,
                 square_send, square_recv, row_send, row_recv, column_send, column_recv):
    dp, tensor = lax.axis_index("dp"), lax.axis_index("tensor")
    rows, columns = weight.shape
    width = columns // 3
    barrier = pltpu.get_barrier_semaphore()

    def greet_rows(step, carry):
        pl.semaphore_signal(barrier, inc=1, device_id=(lax.rem(dp + step, DP), tensor), device_id_type=MESH)
        return carry

    def greet_columns(step, carry):
        pl.semaphore_signal(barrier, inc=1, device_id=(dp, lax.rem(tensor + step, TENSOR)), device_id_type=MESH)
        return carry

    lax.fori_loop(1, DP, greet_rows, 0)
    lax.fori_loop(1, TENSOR, greet_columns, 0)

    inverse_high, inverse_low = halves(inverse[...])
    wide_high, wide_low = halves(wide[...])
    back = dot_nt(wide_high, inverse_high) + dot_nt(wide_low, inverse_high) + dot_nt(wide_high, inverse_low)
    squares = jnp.sum(jnp.sum((back * back).reshape(rows // 8, 8, RANK), axis=0), axis=0, keepdims=True)
    lanes = RANK // 4
    square_inbox[dp] = jnp.concatenate(
        [squares[:, j * lanes:(j + 1) * lanes] for j in range(4)] + [jnp.zeros((4, lanes), jnp.float32)], axis=0
    )
    pl.semaphore_wait(barrier, DP + TENSOR - 2)

    def square_copy(step):
        here = square_inbox.at[dp]
        return remote(here, here, square_send.at[step], square_recv.at[dp], lax.rem(dp + step, DP), tensor)

    def square_begin(step, carry):
        square_copy(step).start()
        return carry

    lax.fori_loop(1, DP, square_begin, 0)
    back_high[...] = back.astype(jnp.bfloat16)
    for j in range(3):
        span = pl.ds(j * width, width)
        ortho = dot_nn(inverse_high, proj[:, span]) + dot_nn(inverse_low, proj[:, span])
        ortho_high[:, span], ortho_low[:, span] = halves(ortho)

    def square_arrive(step, carry):
        source = lax.rem(dp + step, DP)
        there = square_inbox.at[source]
        remote(there, there, square_send.at[0], square_recv.at[source], dp, tensor).wait_recv()
        return carry

    lax.fori_loop(1, DP, square_arrive, 0)
    total = square_inbox[0]
    for source in range(1, DP):
        total += square_inbox[source]
    colsq = jnp.concatenate([total[j:j + 1, :] for j in range(4)], axis=1)
    fresh = back / jnp.sqrt(colsq + epsilon)
    new_basis[...] = fresh
    basis_high[...], basis_low[...] = halves(fresh)

    factor = step_size * math.sqrt(FF / D)
    shift = lax.rem(3 * dp, 4)
    for j in range(3):
        span = pl.ds(j * width, width)
        product = (
            dot_nn(basis_high[...], ortho_high[:, span])
            + dot_nn(basis_low[...], ortho_high[:, span])
            + dot_nn(basis_high[...], ortho_low[:, span])
        )
        update[:, span] = weight[:, span].astype(jnp.float32) - factor * product

    def row_copy(step):
        to = lax.rem(dp + step, DP)
        return remote(row_out.at[to], row_in.at[dp], row_send.at[step], row_recv.at[dp], to, tensor)

    def column_copy(step):
        to = lax.rem(tensor + step, TENSOR)
        return remote(column_out.at[to], column_in.at[tensor], column_send.at[step], column_recv.at[tensor], dp, to)

    def row_begin(step, carry):
        row_copy(step).start()
        return carry

    def column_begin(step, carry):
        column_copy(step).start()
        return carry

    column_out[...] = jnp.zeros(column_out.shape, jnp.bfloat16)
    row_out[...] = jnp.zeros(row_out.shape, jnp.bfloat16)
    pieces = rows // TURN
    for i in range(pieces + 1):
        to = pl.ds(pl.multiple_of(TURN * lax.rem(i + shift, pieces + 1), TURN), TURN)
        turned[to, :] = update[pl.ds(TURN * i, TURN), :] if i < pieces else jnp.zeros((TURN, columns), jnp.float32)
    for to in range(TENSOR):
        column_out[to, pl.ds(0, COLUMNS_OUT), :] = update[pl.ds(COLUMNS_OUT * to, COLUMNS_OUT), :].astype(jnp.bfloat16)
    lax.fori_loop(1, TENSOR, column_begin, 0)
    for j in range(columns // TILE):
        flipped[pl.ds(TILE * j, TILE), :] = jnp.transpose(turned[:, pl.ds(TILE * j, TILE)])
    for to in range(DP):
        row_out[to, pl.ds(0, ROWS_OUT), :] = flipped[pl.ds(ROWS_OUT * to, ROWS_OUT), :].astype(jnp.bfloat16)
    lax.fori_loop(1, DP, row_begin, 0)
    column_in[tensor] = column_out[tensor]
    row_in[dp] = row_out[dp]

    for j in range(3):
        span = pl.ds(j * width, width)
        product = dot_nn(back_high[...], ortho_high[:, span])
        new_momentum[:, span] = momentum[:, span] + gradient[:, span].astype(jnp.float32) - (1.0 - decay_rate) * product

    def column_arrive(step, carry):
        source = lax.rem(tensor + step, TENSOR)
        there = column_in.at[source]
        remote(there, there, column_send.at[0], column_recv.at[source], dp, tensor).wait_recv()
        return carry

    def row_arrive(step, carry):
        source = lax.rem(dp + step, DP)
        there = row_in.at[source]
        remote(there, there, row_send.at[0], row_recv.at[source], dp, tensor).wait_recv()
        return carry

    def scaled(tile):
        largest = jnp.max(jnp.abs(tile), axis=1, keepdims=True)
        return (tile * (1.0 / (largest + epsilon))).astype(jnp.bfloat16), largest

    lax.fori_loop(1, TENSOR, column_arrive, 0)
    count = columns // TILE
    lane_of = lax.broadcasted_iota(jnp.int32, (16, 256), 1)
    scales = jnp.zeros((16, 256), jnp.float32)
    for source in range(TENSOR):
        for j in range(count):
            values, largest = scaled(column_in[source, :, pl.ds(TILE * j, TILE)].astype(jnp.float32))
            column_values[:, pl.ds(columns * source + TILE * j, TILE)] = values[:COLUMNS_OUT]
            scales = jnp.where(lane_of == count * source + j, largest, scales)
    column_scales[...] = scales[:COLUMNS_OUT, :FF // TILE]

    lax.fori_loop(1, DP, row_arrive, 0)
    lane_of = lax.broadcasted_iota(jnp.int32, (CHUNK, TILE), 1)
    scales = jnp.zeros((CHUNK, TILE), jnp.float32)
    for tile in range(D // TILE):
        source = TILE * tile // rows
        part = lambda which: row_in[which, :, pl.ds(TILE * ((tile - rows * which // TILE) % 2), TILE)].astype(jnp.float32)
        block = part(source)
        bound = rows * (source + 1) - TILE * tile
        if bound < TILE:
            block = jnp.where(lane_of < bound, block, part(source + 1))
        values, largest = scaled(block)
        row_values[:, pl.ds(TILE * tile, TILE)] = values[:ROWS_OUT]
        scales = jnp.where(lane_of == tile, largest, scales)
    row_scales[...] = scales[:ROWS_OUT, :D // TILE]

    def square_drain(step, carry):
        square_copy(step).wait_send()
        row_copy(step).wait_send()
        return carry

    def column_drain(step, carry):
        column_copy(step).wait_send()
        return carry

    lax.fori_loop(1, DP, square_drain, 0)
    lax.fori_loop(1, TENSOR, column_drain, 0)


def apply_update(weight, momentum, gradient, wide, inverse, proj):
    rows, columns = weight.shape
    dma = pltpu.SemaphoreType.DMA
    f32, bf16 = jnp.float32, jnp.bfloat16
    shape = jax.ShapeDtypeStruct
    return pl.pallas_call(
        apply_kernel,
        out_shape=(
            shape((rows, columns), f32),
            shape((rows, RANK), f32),
            shape((ROWS_OUT, D), bf16),
            shape((ROWS_OUT, D // TILE), f32),
            shape((COLUMNS_OUT, FF), bf16),
            shape((COLUMNS_OUT, FF // TILE), f32),
        ),
        in_specs=[VMEM] * 6,
        out_specs=(VMEM,) * 6,
        scratch_shapes=[
            pltpu.VMEM((rows, RANK), bf16),
            pltpu.VMEM((rows, RANK), bf16),
            pltpu.VMEM((rows, RANK), bf16),
            pltpu.VMEM((RANK, columns), bf16),
            pltpu.VMEM((RANK, columns), bf16),
            pltpu.VMEM((DP, 8, RANK // 4), f32),
            pltpu.VMEM((rows, columns), f32),
            pltpu.VMEM((rows + TURN, columns), f32),
            pltpu.VMEM((columns, rows + TURN), f32),
            pltpu.VMEM((DP, CHUNK, rows + TURN), bf16),
            pltpu.VMEM((DP, CHUNK, rows + TURN), bf16),
            pltpu.VMEM((TENSOR, 16, columns), bf16),
            pltpu.VMEM((TENSOR, 16, columns), bf16),
            dma((DP,)), dma((DP,)), dma((DP,)), dma((DP,)), dma((TENSOR,)), dma((TENSOR,)),
        ],
        compiler_params=pltpu.CompilerParams(collective_id=2, has_side_effects=True, vmem_limit_bytes=48 << 20),
    )(weight, momentum, gradient, wide, inverse, proj)


def on_device(weight, gradient, momentum, basis):
    proj = proj_transposed(momentum, gradient, basis)
    gram, wide = gram_and_wide(momentum, gradient, proj)
    inverse = inverse_factor(gram)
    return apply_update(weight, momentum, gradient, wide, inverse, proj)


def solution(mesh):
    placed = (P("dp", "tensor"), P("dp", "tensor"), P("dp", "tensor"), P("dp", None))
    return jax.shard_map(
        on_device,
        mesh=mesh,
        in_specs=placed,
        out_specs=(
            P("dp", "tensor"),
            P("dp", None),
            P(("tensor", "dp"), None),
            P(("tensor", "dp"), None),
            P(("dp", "tensor"), None),
            P(("dp", "tensor"), None),
        ),
        check_vma=False,
    )
```

```python
import functools
import math

import jax
import jax.numpy as jnp
from jax import lax
from jax.experimental import pallas as pl
from jax.experimental.pallas import tpu as pltpu
from jax.sharding import PartitionSpec as P

RANK = 512
BLOCK = 128
STRIP = 8
HIGHEST = lax.Precision.HIGHEST


def dot_nt(a, b, precision=None):
    return lax.dot_general(a, b, (((1,), (1,)), ((), ())), precision=precision, preferred_element_type=jnp.float32)


def dot_nn(a, b, precision=None):
    return lax.dot_general(a, b, (((1,), (0,)), ((), ())), precision=precision, preferred_element_type=jnp.float32)


def invert_block(tiles):
    shape = (STRIP, BLOCK)
    count = BLOCK // STRIP
    row_of = lax.broadcasted_iota(jnp.int32, shape, 0)
    lane_of = lax.broadcasted_iota(jnp.int32, shape, 1)
    tiles = list(tiles)
    own = [jnp.where(lane_of == row_of + STRIP * i, 1.0, 0.0).astype(jnp.float32) for i in range(count)]
    for s in range(count):
        spread = lambda tile, m, lane: jnp.broadcast_to(tile[m:m + 1, lane:lane + 1], shape)
        small = [[spread(tiles[s], m, STRIP * s + k) for k in range(m + 1)] for m in range(STRIP)]
        rows = [jnp.broadcast_to(tiles[s][m:m + 1, :], shape) for m in range(STRIP)]
        extra = [jnp.broadcast_to(own[s][m:m + 1, :], shape) for m in range(STRIP)]
        factor = [[None] * STRIP for _ in range(STRIP)]
        inverse, root = [], []
        for k in range(STRIP):
            r = lax.rsqrt(small[k][k])
            root.append(r)
            inverse.append(r * r)
            for m in range(k + 1, STRIP):
                f = small[m][k] * inverse[k]
                factor[m][k] = f
                for j in range(k + 1, m + 1):
                    small[m][j] = small[m][j] - f * small[j][k]
                rows[m] = rows[m] - f * rows[k]
                extra[m] = extra[m] - f * extra[k]
        for i in range(s + 1, count):
            cols = [jnp.broadcast_to(tiles[i][:, STRIP * s + k:STRIP * s + k + 1], shape) for k in range(STRIP)]
            for k in range(STRIP):
                for m in range(k + 1, STRIP):
                    cols[m] = cols[m] - cols[k] * factor[m][k]
            for k in range(STRIP):
                g = cols[k] * inverse[k]
                tiles[i] = tiles[i] - g * rows[k]
                own[i] = own[i] - g * extra[k]
        done = extra[0] * root[0]
        for m in range(1, STRIP):
            done = jnp.where(row_of == m, extra[m] * root[m], done)
        own[s] = done
    return own


def factor_and_invert(inv_ref, a_ref, small_ref):
    rank = a_ref.shape[0]
    row_of = lax.broadcasted_iota(jnp.int32, (rank, rank), 0)
    inv_ref[...] = jnp.where(row_of == lax.broadcasted_iota(jnp.int32, (rank, rank), 1), 1.0, 0.0).astype(jnp.float32)

    def step(b, carry):
        at = pl.multiple_of(b * BLOCK, BLOCK)
        tiles = [a_ref[pl.ds(pl.multiple_of(at + STRIP * i, STRIP), STRIP), pl.ds(at, BLOCK)] for i in range(BLOCK // STRIP)]
        own = invert_block(tiles)
        for i, tile in enumerate(own):
            small_ref[pl.ds(STRIP * i, STRIP), :] = tile
        inverse = small_ref[...]
        rows = dot_nn(inverse, inv_ref[pl.ds(at, BLOCK), :], HIGHEST)
        below = lax.broadcasted_iota(jnp.int32, (rank, BLOCK), 0) >= at + BLOCK
        panel = jnp.where(below, dot_nt(a_ref[:, pl.ds(at, BLOCK)], inverse, HIGHEST), 0.0)
        inv_ref[pl.ds(at, BLOCK), :] = rows
        a_ref[...] -= dot_nt(panel, panel, HIGHEST)
        inv_ref[...] -= dot_nn(panel, rows, HIGHEST)
        return carry

    lax.fori_loop(0, rank // BLOCK, step, 0)


D = 7168
FF = 18432
TILE = 128
decay_rate = 0.95
step_size = 0.3
epsilon = 1e-06

DP = 32
TENSOR = 16
CHIPS = 16
SLAB = RANK // DP
MESH = pl.DeviceIdType.MESH
VMEM = pl.BlockSpec(memory_space=pltpu.VMEM)


def halves(x):
    high = x.astype(jnp.bfloat16)
    return high, (x - high.astype(jnp.float32)).astype(jnp.bfloat16)


def remote(src, dst, send, recv, dp, tensor):
    return pltpu.make_async_remote_copy(
        src_ref=src, dst_ref=dst, send_sem=send, recv_sem=recv, device_id=(dp, tensor), device_id_type=MESH
    )


def slab_rows(dp):
    return pl.ds(pl.multiple_of(SLAB * (CHIPS * lax.rem(dp, 2) + dp // 2), SLAB), SLAB)


LONG = CHIPS // 2


def spread_slabs(slab, dp, tensor, recv, ring_send, cross_send, pass_send, pass_recv):
    core, chip = lax.rem(dp, 2), dp // 2
    side, z = chip // LONG, lax.rem(chip, LONG)
    other = dp + 1 - 2 * core
    started = []

    def at(which_side, offset):
        return LONG * which_side + lax.rem(z + offset + LONG, LONG)

    def mine(source):
        return slab(2 * source + core)

    def send(source, target, sem):
        copy = remote(mine(source), mine(source), sem, recv.at[source], 2 * target + core, tensor)
        copy.start()
        started.append(copy)

    def hand_over(source):
        copy = remote(mine(source), mine(source), pass_send.at[source], pass_recv.at[source], other, tensor)
        copy.start()
        started.append(copy)

    def arrived(source):
        remote(mine(source), mine(source), ring_send.at[0], recv.at[source], other, tensor).wait_recv()

    across = at(1 - side, 0)
    offsets = [4, 3, -3, 2, -2, 1, -1]
    for offset in offsets:
        send(chip, at(side, offset), ring_send.at[offset % LONG])
    send(chip, across, cross_send.at[0])
    hand_over(chip)
    for offset in reversed(offsets):
        source = at(side, offset)
        arrived(source)
        send(source, across, cross_send.at[offset % LONG])
        hand_over(source)
    for offset in [0] + offsets[::-1]:
        source = at(1 - side, offset)
        arrived(source)
        hand_over(source)

    def passed(step, carry):
        source = lax.rem(chip + step, CHIPS)
        there = slab(2 * source + 1 - core)
        remote(there, there, pass_send.at[source], pass_recv.at[source], other, tensor).wait_recv()
        return carry

    lax.fori_loop(0, CHIPS, passed, 0)
    return started


def greet_dp(barrier, dp, tensor):
    core, chip = lax.rem(dp, 2), dp // 2

    def greet(step, carry):
        to = lax.rem(chip + step, CHIPS)
        pl.semaphore_signal(barrier, inc=1, device_id=(2 * to + core, tensor), device_id_type=MESH)
        return carry

    lax.fori_loop(1, CHIPS, greet, 0)
    pl.semaphore_signal(barrier, inc=1, device_id=(dp + 1 - 2 * core, tensor), device_id_type=MESH)


OWNERS = 5
TALL = RANK // 8
WIDE_ROWS, WIDE_COLUMNS = 64, 128


def factor_kernel(momentum, gradient, basis, proj, wide, inverse, high, low, basis_high, basis_low, pair_out, pair_in, part, inbox,
                  gram, work, block, gram_part, gram_inbox, wide_part, wide_inbox, wide_all, pair_sems, send, recv,
                  tile_send, tile_recv, back_send, back_recv, wide_send, wide_recv, out_send, out_recv, *gather_sems):
    proj_sems, gram_sems = gather_sems[:len(gather_sems) // 2], gather_sems[len(gather_sems) // 2:]
    dp, tensor = lax.axis_index("dp"), lax.axis_index("tensor")
    core, chip = lax.rem(dp, 2), dp // 2
    other = dp + 1 - 2 * core
    half = RANK // 2
    rows, columns = momentum.shape
    width = columns // 3

    barrier = pltpu.get_barrier_semaphore()
    greet_dp(barrier, dp, tensor)

    def greet(step, carry):
        to = lax.rem(tensor + step, TENSOR)
        pl.semaphore_signal(barrier, inc=1, device_id=(dp, to), device_id_type=MESH)
        return carry

    lax.fori_loop(1, TENSOR, greet, 0)

    for j in range(3):
        span = pl.ds(j * width, width)
        high[:, span], low[:, span] = halves(momentum[:, span] + gradient[:, span].astype(jnp.float32))
    basis_high[...], basis_low[...] = halves(jnp.transpose(basis[...]))

    def product(first, j):
        span = pl.ds(j * width, width)
        rows = pl.ds(pl.multiple_of(first, half), half)
        return (
            dot_nn(basis_high[rows, :], high[:, span])
            + dot_nn(basis_high[rows, :], low[:, span])
            + dot_nn(basis_low[rows, :], high[:, span])
        )

    for j in range(3):
        pair_out[:, pl.ds(j * width, width)] = product((1 - core) * half, j)
    pl.semaphore_wait(barrier, CHIPS + TENSOR - 1)
    swap = remote(pair_out, pair_in, pair_sems.at[0], pair_sems.at[1], other, tensor)
    swap.start()
    mine = [product(core * half, j) for j in range(3)]
    swap.wait_recv()
    for j in range(3):
        span = pl.ds(j * width, width)
        part[:, span] = (mine[j] + pair_in[:, span]).astype(jnp.bfloat16)

    def slab(which):
        return part.at[pl.ds(pl.multiple_of(which * SLAB, SLAB), SLAB), :]

    def slab_copy(step):
        to = lax.rem(chip + step, CHIPS)
        return remote(slab(to), inbox.at[chip], send.at[step], recv.at[chip], 2 * to + core, tensor)

    def slab_begin(step, carry):
        slab_copy(step).start()
        return carry

    def slab_arrive(step, total):
        source = lax.rem(chip + CHIPS - step, CHIPS)
        remote(inbox.at[source], inbox.at[source], send.at[0], recv.at[source], other, tensor).wait_recv()
        return total + inbox[source].astype(jnp.float32)

    def slab_drain(step, carry):
        slab_copy(step).wait_send()
        return carry

    lax.fori_loop(1, CHIPS, slab_begin, 0)
    total = part[pl.ds(pl.multiple_of(chip * SLAB, SLAB), SLAB), :].astype(jnp.float32)
    total = lax.fori_loop(1, CHIPS, slab_arrive, total)
    proj[slab_rows(dp), :] = total.astype(jnp.bfloat16)
    proj_sends = spread_slabs(lambda which: proj.at[slab_rows(which), :], dp, tensor, *proj_sems)

    def tile_row(which):
        both = dot_nt(proj[pl.ds(pl.multiple_of(16 * (which // 2), 16), 16), :], proj[...])
        return jnp.where(lax.rem(which, 2) == 0, both[:8], both[8:])

    upper, lower = tile_row(dp), tile_row(TALL - 1 - dp)
    column = lambda x, j: x[:, BLOCK * j:BLOCK * (j + 1)]
    short = dp < TALL // 4
    gram_part[0] = column(upper, 0)
    gram_part[1] = jnp.where(short, column(lower, 0), column(upper, 1))
    for j in range(2, OWNERS):
        gram_part[j] = jnp.where(short, column(lower, j - 1), column(lower, j - 2))

    def tile_copy(owner):
        return remote(gram_part.at[owner], gram_inbox.at[tensor], tile_send.at[owner], tile_recv.at[tensor], dp, owner)

    def tile_begin(owner, carry):
        @pl.when(owner != tensor)
        def _():
            tile_copy(owner).start()

        return carry

    lax.fori_loop(0, OWNERS, tile_begin, 0)
    work[:rows, :] = dot_nt(high[...], proj[...])

    def back_copy(step):
        to = lax.rem(tensor + step, TENSOR)
        here = gram.at[dp, tensor]
        return remote(here, here, back_send.at[step], back_recv.at[tensor], dp, to)

    @pl.when(tensor < OWNERS)
    def _():
        def arrive(step, total):
            source = lax.rem(tensor + step, TENSOR)
            there = gram_inbox.at[source]
            remote(there, there, tile_send.at[0], tile_recv.at[source], dp, tensor).wait_recv()
            return total + gram_inbox[source]

        def back_begin(step, carry):
            back_copy(step).start()
            return carry

        gram[dp, tensor] = lax.fori_loop(1, TENSOR, arrive, gram_part[tensor])
        lax.fori_loop(1, TENSOR, back_begin, 0)

    wide_part[:rows, :] = (work[:rows, :] + dot_nt(low[...], proj[...])).astype(jnp.bfloat16)
    wide_part[rows:, :] = jnp.zeros((wide_part.shape[0] - rows, RANK), jnp.bfloat16)

    def piece(ref, which):
        return ref.at[
            pl.ds(pl.multiple_of(WIDE_ROWS * (which // 4), WIDE_ROWS), WIDE_ROWS),
            pl.ds(pl.multiple_of(WIDE_COLUMNS * lax.rem(which, 4), WIDE_COLUMNS), WIDE_COLUMNS),
        ]

    def wide_copy(step):
        to = lax.rem(tensor + step, TENSOR)
        return remote(piece(wide_part, to), wide_inbox.at[tensor], wide_send.at[step], wide_recv.at[tensor], dp, to)

    def wide_begin(step, carry):
        wide_copy(step).start()
        return carry

    lax.fori_loop(1, TENSOR, wide_begin, 0)

    def wide_arrive(step, total):
        source = lax.rem(tensor + step, TENSOR)
        there = wide_inbox.at[source]
        remote(there, there, wide_send.at[0], wide_recv.at[source], dp, tensor).wait_recv()
        return total + wide_inbox[source].astype(jnp.float32)

    def out_copy(step):
        to = lax.rem(tensor + step, TENSOR)
        here = piece(wide_all, tensor)
        return remote(here, here, out_send.at[step], out_recv.at[tensor], dp, to)

    def out_begin(step, carry):
        out_copy(step).start()
        return carry

    def back_arrive(owner, carry):
        @pl.when(owner != tensor)
        def _():
            there = gram.at[dp, owner]
            remote(there, there, back_send.at[0], back_recv.at[owner], dp, tensor).wait_recv()

        return carry

    lax.fori_loop(0, OWNERS, back_arrive, 0)
    gram_sends = spread_slabs(lambda which: gram.at[which], dp, tensor, *gram_sems)
    work[...] = jnp.zeros_like(work)
    for i in range(DP):
        places = [(r, j) for r in (i, TALL - 1 - i) for j in range(8 * r // BLOCK + 1)]
        for j, (r, c) in enumerate(places):
            work[pl.ds(8 * r, 8), pl.ds(BLOCK * c, BLOCK)] = gram[i, j]
    piece(wide_all, tensor)[...] = lax.fori_loop(
        1, TENSOR, wide_arrive, piece(wide_part, tensor)[...].astype(jnp.float32)
    )
    lax.fori_loop(1, TENSOR, out_begin, 0)
    factor_and_invert(inverse, work, block)

    def out_arrive(step, carry):
        source = lax.rem(tensor + step, TENSOR)
        there = piece(wide_all, source)
        remote(there, there, out_send.at[0], out_recv.at[source], dp, tensor).wait_recv()
        return carry

    lax.fori_loop(1, TENSOR, out_arrive, 0)
    wide[...] = wide_all[:rows, :]

    def tile_drain(owner, carry):
        @pl.when(owner != tensor)
        def _():
            tile_copy(owner).wait_send()

        return carry

    def drain(step, carry):
        wide_copy(step).wait_send()
        out_copy(step).wait_send()

        @pl.when(tensor < OWNERS)
        def _():
            back_copy(step).wait_send()

        return carry

    for copy in proj_sends + gram_sends:
        copy.wait_send()
    swap.wait_send()
    lax.fori_loop(1, CHIPS, slab_drain, 0)
    lax.fori_loop(0, OWNERS, tile_drain, 0)
    lax.fori_loop(1, TENSOR, drain, 0)


def factor(momentum, gradient, basis):
    rows, columns = momentum.shape
    half = RANK // 2
    padded = TENSOR // 4 * WIDE_ROWS
    dma = pltpu.SemaphoreType.DMA
    f32, bf16 = jnp.float32, jnp.bfloat16
    gather = [dma((CHIPS,)), dma((LONG,)), dma((LONG,)), dma((CHIPS,)), dma((CHIPS,))]
    return pl.pallas_call(
        factor_kernel,
        out_shape=(
            jax.ShapeDtypeStruct((RANK, columns), bf16),
            jax.ShapeDtypeStruct((rows, RANK), f32),
            jax.ShapeDtypeStruct((RANK, RANK), f32),
        ),
        in_specs=[VMEM] * 3,
        out_specs=(VMEM,) * 3,
        scratch_shapes=[
            pltpu.VMEM((rows, columns), bf16),
            pltpu.VMEM((rows, columns), bf16),
            pltpu.VMEM((RANK, rows), bf16),
            pltpu.VMEM((RANK, rows), bf16),
            pltpu.VMEM((half, columns), f32),
            pltpu.VMEM((half, columns), f32),
            pltpu.VMEM((half, columns), bf16),
            pltpu.VMEM((CHIPS, SLAB, columns), bf16),
            pltpu.VMEM((DP, OWNERS, 8, BLOCK), f32),
            pltpu.VMEM((RANK, RANK), f32),
            pltpu.VMEM((BLOCK, BLOCK), f32),
            pltpu.VMEM((OWNERS, 8, BLOCK), f32),
            pltpu.VMEM((TENSOR, 8, 128), f32),
            pltpu.VMEM((padded, RANK), bf16),
            pltpu.VMEM((TENSOR, WIDE_ROWS, WIDE_COLUMNS), bf16),
            pltpu.VMEM((padded, RANK), f32),
            dma((2,)), dma((CHIPS,)), dma((CHIPS,)),
            dma((OWNERS,)), dma((TENSOR,)), dma((TENSOR,)), dma((OWNERS,)),
            dma((TENSOR,)), dma((TENSOR,)), dma((TENSOR,)), dma((TENSOR,)),
        ] + gather + gather,
        compiler_params=pltpu.CompilerParams(collective_id=0, has_side_effects=True, vmem_limit_bytes=48 << 20),
    )(momentum, gradient, basis)


CHUNK = 48
ROWS_OUT = FF // TENSOR // DP
COLUMNS_OUT = D // DP // TENSOR
TURN = 32


def apply_kernel(weight, momentum, gradient, wide, inverse, proj,
                 new_momentum, new_basis, row_values, row_scales, column_values, column_scales,
                 back_high, basis_high, basis_low, ortho_high, ortho_low, square_inbox, update, turned, flipped, row_out, row_in, column_out, column_in,
                 square_send, square_recv, row_send, row_recv, column_send, column_recv):
    dp, tensor = lax.axis_index("dp"), lax.axis_index("tensor")
    rows, columns = weight.shape
    width = columns // 3
    barrier = pltpu.get_barrier_semaphore()

    def greet_rows(step, carry):
        pl.semaphore_signal(barrier, inc=1, device_id=(lax.rem(dp + step, DP), tensor), device_id_type=MESH)
        return carry

    def greet_columns(step, carry):
        pl.semaphore_signal(barrier, inc=1, device_id=(dp, lax.rem(tensor + step, TENSOR)), device_id_type=MESH)
        return carry

    lax.fori_loop(1, DP, greet_rows, 0)
    lax.fori_loop(1, TENSOR, greet_columns, 0)

    inverse_high, inverse_low = halves(inverse[...])
    wide_high, wide_low = halves(wide[...])
    back = dot_nt(wide_high, inverse_high) + dot_nt(wide_low, inverse_high) + dot_nt(wide_high, inverse_low)
    squares = jnp.sum(jnp.sum((back * back).reshape(rows // 8, 8, RANK), axis=0), axis=0, keepdims=True)
    lanes = RANK // 4
    square_inbox[dp] = jnp.concatenate(
        [squares[:, j * lanes:(j + 1) * lanes] for j in range(4)] + [jnp.zeros((4, lanes), jnp.float32)], axis=0
    )
    pl.semaphore_wait(barrier, DP + TENSOR - 2)

    def square_copy(step):
        here = square_inbox.at[dp]
        return remote(here, here, square_send.at[step], square_recv.at[dp], lax.rem(dp + step, DP), tensor)

    def square_begin(step, carry):
        square_copy(step).start()
        return carry

    lax.fori_loop(1, DP, square_begin, 0)
    back_high[...] = back.astype(jnp.bfloat16)
    for j in range(3):
        span = pl.ds(j * width, width)
        ortho = dot_nn(inverse_high, proj[:, span]) + dot_nn(inverse_low, proj[:, span])
        ortho_high[:, span], ortho_low[:, span] = halves(ortho)

    def square_arrive(step, carry):
        source = lax.rem(dp + step, DP)
        there = square_inbox.at[source]
        remote(there, there, square_send.at[0], square_recv.at[source], dp, tensor).wait_recv()
        return carry

    lax.fori_loop(1, DP, square_arrive, 0)
    total = square_inbox[0]
    for source in range(1, DP):
        total += square_inbox[source]
    colsq = jnp.concatenate([total[j:j + 1, :] for j in range(4)], axis=1)
    fresh = back / jnp.sqrt(colsq + epsilon)
    new_basis[...] = fresh
    basis_high[...], basis_low[...] = halves(fresh)

    factor = step_size * math.sqrt(FF / D)
    shift = lax.rem(3 * dp, 4)
    for j in range(3):
        span = pl.ds(j * width, width)
        product = (
            dot_nn(basis_high[...], ortho_high[:, span])
            + dot_nn(basis_low[...], ortho_high[:, span])
            + dot_nn(basis_high[...], ortho_low[:, span])
        )
        update[:, span] = weight[:, span].astype(jnp.float32) - factor * product

    def row_copy(step):
        to = lax.rem(dp + step, DP)
        return remote(row_out.at[to], row_in.at[dp], row_send.at[step], row_recv.at[dp], to, tensor)

    def column_copy(step):
        to = lax.rem(tensor + step, TENSOR)
        return remote(column_out.at[to], column_in.at[tensor], column_send.at[step], column_recv.at[tensor], dp, to)

    def row_begin(step, carry):
        row_copy(step).start()
        return carry

    def column_begin(step, carry):
        column_copy(step).start()
        return carry

    column_out[...] = jnp.zeros(column_out.shape, jnp.bfloat16)
    row_out[...] = jnp.zeros(row_out.shape, jnp.bfloat16)
    pieces = rows // TURN
    for i in range(pieces + 1):
        to = pl.ds(pl.multiple_of(TURN * lax.rem(i + shift, pieces + 1), TURN), TURN)
        turned[to, :] = update[pl.ds(TURN * i, TURN), :] if i < pieces else jnp.zeros((TURN, columns), jnp.float32)
    for to in range(TENSOR):
        column_out[to, pl.ds(0, COLUMNS_OUT), :] = update[pl.ds(COLUMNS_OUT * to, COLUMNS_OUT), :].astype(jnp.bfloat16)
    lax.fori_loop(1, TENSOR, column_begin, 0)
    for j in range(columns // TILE):
        flipped[pl.ds(TILE * j, TILE), :] = jnp.transpose(turned[:, pl.ds(TILE * j, TILE)])
    for to in range(DP):
        row_out[to, pl.ds(0, ROWS_OUT), :] = flipped[pl.ds(ROWS_OUT * to, ROWS_OUT), :].astype(jnp.bfloat16)
    lax.fori_loop(1, DP, row_begin, 0)
    column_in[tensor] = column_out[tensor]
    row_in[dp] = row_out[dp]

    for j in range(3):
        span = pl.ds(j * width, width)
        product = dot_nn(back_high[...], ortho_high[:, span])
        new_momentum[:, span] = momentum[:, span] + gradient[:, span].astype(jnp.float32) - (1.0 - decay_rate) * product

    def column_arrive(step, carry):
        source = lax.rem(tensor + step, TENSOR)
        there = column_in.at[source]
        remote(there, there, column_send.at[0], column_recv.at[source], dp, tensor).wait_recv()
        return carry

    def row_arrive(step, carry):
        source = lax.rem(dp + step, DP)
        there = row_in.at[source]
        remote(there, there, row_send.at[0], row_recv.at[source], dp, tensor).wait_recv()
        return carry

    def scaled(tile):
        largest = jnp.max(jnp.abs(tile), axis=1, keepdims=True)
        return (tile * (1.0 / (largest + epsilon))).astype(jnp.bfloat16), largest

    lax.fori_loop(1, TENSOR, column_arrive, 0)
    count = columns // TILE
    lane_of = lax.broadcasted_iota(jnp.int32, (16, 256), 1)
    scales = jnp.zeros((16, 256), jnp.float32)
    for source in range(TENSOR):
        for j in range(count):
            values, largest = scaled(column_in[source, :, pl.ds(TILE * j, TILE)].astype(jnp.float32))
            column_values[:, pl.ds(columns * source + TILE * j, TILE)] = values[:COLUMNS_OUT]
            scales = jnp.where(lane_of == count * source + j, largest, scales)
    column_scales[...] = scales[:COLUMNS_OUT, :FF // TILE]

    lax.fori_loop(1, DP, row_arrive, 0)
    lane_of = lax.broadcasted_iota(jnp.int32, (CHUNK, TILE), 1)
    scales = jnp.zeros((CHUNK, TILE), jnp.float32)
    for tile in range(D // TILE):
        source = TILE * tile // rows
        part = lambda which: row_in[which, :, pl.ds(TILE * ((tile - rows * which // TILE) % 2), TILE)].astype(jnp.float32)
        block = part(source)
        bound = rows * (source + 1) - TILE * tile
        if bound < TILE:
            block = jnp.where(lane_of < bound, block, part(source + 1))
        values, largest = scaled(block)
        row_values[:, pl.ds(TILE * tile, TILE)] = values[:ROWS_OUT]
        scales = jnp.where(lane_of == tile, largest, scales)
    row_scales[...] = scales[:ROWS_OUT, :D // TILE]

    def square_drain(step, carry):
        square_copy(step).wait_send()
        row_copy(step).wait_send()
        return carry

    def column_drain(step, carry):
        column_copy(step).wait_send()
        return carry

    lax.fori_loop(1, DP, square_drain, 0)
    lax.fori_loop(1, TENSOR, column_drain, 0)


def apply_update(weight, momentum, gradient, wide, inverse, proj):
    rows, columns = weight.shape
    dma = pltpu.SemaphoreType.DMA
    f32, bf16 = jnp.float32, jnp.bfloat16
    shape = jax.ShapeDtypeStruct
    return pl.pallas_call(
        apply_kernel,
        out_shape=(
            shape((rows, columns), f32),
            shape((rows, RANK), f32),
            shape((ROWS_OUT, D), bf16),
            shape((ROWS_OUT, D // TILE), f32),
            shape((COLUMNS_OUT, FF), bf16),
            shape((COLUMNS_OUT, FF // TILE), f32),
        ),
        in_specs=[VMEM] * 6,
        out_specs=(VMEM,) * 6,
        scratch_shapes=[
            pltpu.VMEM((rows, RANK), bf16),
            pltpu.VMEM((rows, RANK), bf16),
            pltpu.VMEM((rows, RANK), bf16),
            pltpu.VMEM((RANK, columns), bf16),
            pltpu.VMEM((RANK, columns), bf16),
            pltpu.VMEM((DP, 8, RANK // 4), f32),
            pltpu.VMEM((rows, columns), f32),
            pltpu.VMEM((rows + TURN, columns), f32),
            pltpu.VMEM((columns, rows + TURN), f32),
            pltpu.VMEM((DP, CHUNK, rows + TURN), bf16),
            pltpu.VMEM((DP, CHUNK, rows + TURN), bf16),
            pltpu.VMEM((TENSOR, 16, columns), bf16),
            pltpu.VMEM((TENSOR, 16, columns), bf16),
            dma((DP,)), dma((DP,)), dma((DP,)), dma((DP,)), dma((TENSOR,)), dma((TENSOR,)),
        ],
        compiler_params=pltpu.CompilerParams(collective_id=1, has_side_effects=True, vmem_limit_bytes=48 << 20),
    )(weight, momentum, gradient, wide, inverse, proj)


def on_device(weight, gradient, momentum, basis):
    proj, wide, inverse = factor(momentum, gradient, basis)
    return apply_update(weight, momentum, gradient, wide, inverse, proj)


def solution(mesh):
    placed = (P("dp", "tensor"), P("dp", "tensor"), P("dp", "tensor"), P("dp", None))
    return jax.shard_map(
        on_device,
        mesh=mesh,
        in_specs=placed,
        out_specs=(
            P("dp", "tensor"),
            P("dp", None),
            P(("tensor", "dp"), None),
            P(("tensor", "dp"), None),
            P(("dp", "tensor"), None),
            P(("dp", "tensor"), None),
        ),
        check_vma=False,
    )
```

```python
import math

import jax
import jax.numpy as jnp
from jax import lax
from jax.experimental import pallas as pl
from jax.experimental.pallas import tpu as pltpu
from jax.sharding import PartitionSpec as P

RANK = 512
BLOCK = 128
STRIP = 8


def dot_nt(a, b):
    return lax.dot_general(a, b, (((1,), (1,)), ((), ())), preferred_element_type=jnp.float32)


def dot_nn(a, b):
    return lax.dot_general(a, b, (((1,), (0,)), ((), ())), preferred_element_type=jnp.float32)


def invert_block(tiles):
    shape = (STRIP, BLOCK)
    count = BLOCK // STRIP
    row_of = lax.broadcasted_iota(jnp.int32, shape, 0)
    lane_of = lax.broadcasted_iota(jnp.int32, shape, 1)
    tiles = list(tiles)
    own = [jnp.where(lane_of == row_of + STRIP * i, 1.0, 0.0).astype(jnp.float32) for i in range(count)]
    for s in range(count):
        spread = lambda tile, m, lane: jnp.broadcast_to(tile[m:m + 1, lane:lane + 1], shape)
        small = [[spread(tiles[s], m, STRIP * s + k) for k in range(m + 1)] for m in range(STRIP)]
        rows = [jnp.broadcast_to(tiles[s][m:m + 1, :], shape) for m in range(STRIP)]
        extra = [jnp.broadcast_to(own[s][m:m + 1, :], shape) for m in range(STRIP)]
        factor = [[None] * STRIP for _ in range(STRIP)]
        inverse, root = [], []
        for k in range(STRIP):
            root.append(lax.rsqrt(small[k][k]))
            inverse.append(1.0 / small[k][k])
            for m in range(k + 1, STRIP):
                f = small[m][k] * inverse[k]
                factor[m][k] = f
                for j in range(k + 1, m + 1):
                    small[m][j] = small[m][j] - (small[m][k] * small[j][k]) * inverse[k]
                rows[m] = rows[m] - f * rows[k]
                extra[m] = extra[m] - f * extra[k]
        for i in range(s + 1, count):
            cols = [jnp.broadcast_to(tiles[i][:, STRIP * s + k:STRIP * s + k + 1], shape) for k in range(STRIP)]
            for k in range(STRIP):
                for m in range(k + 1, STRIP):
                    cols[m] = cols[m] - cols[k] * factor[m][k]
            for k in range(STRIP):
                g = cols[k] * inverse[k]
                tiles[i] = tiles[i] - g * rows[k]
                own[i] = own[i] - g * extra[k]
        done = extra[0] * root[0]
        for m in range(1, STRIP):
            done = jnp.where(row_of == m, extra[m] * root[m], done)
        own[s] = done
    return own


def halves(x):
    high = x.astype(jnp.bfloat16)
    return high, (x - high.astype(jnp.float32)).astype(jnp.bfloat16)


def split_dot(dot, a, b):
    a_high, a_low = halves(a)
    b_high, b_low = halves(b)
    return dot(a_high, b_high) + (dot(a_high, b_low) + dot(a_low, b_high))


def factor_and_invert(inv_ref, a_ref):
    rank = a_ref.shape[0]
    blocks = rank // BLOCK
    span = lambda b: pl.ds(b * BLOCK, BLOCK)
    inv_ref[...] = jnp.zeros_like(inv_ref)
    diagonal = a_ref[span(0), span(0)]
    for b in range(blocks):
        inverse = jnp.concatenate(invert_block([diagonal[STRIP * i:STRIP * (i + 1)] for i in range(BLOCK // STRIP)]), axis=0)
        done, end = pl.ds(0, b * BLOCK), (b + 1) * BLOCK
        rest = pl.ds(end, rank - end)
        if b + 1 < blocks:
            near = split_dot(dot_nt, a_ref[span(b + 1), span(b)], inverse)
            diagonal = a_ref[span(b + 1), span(b + 1)] - split_dot(dot_nt, near, near)
        inv_ref[span(b), span(b)] = inverse
        if b:
            inv_ref[span(b), done] = split_dot(dot_nn, inverse, inv_ref[span(b), done])
        if b + 1 < blocks:
            panel = near
            if b + 2 < blocks:
                far = pl.ds(end + BLOCK, rank - end - BLOCK)
                distant = split_dot(dot_nt, a_ref[far, span(b)], inverse)
                panel = jnp.concatenate([near, distant], axis=0)
                a_ref[far, rest] -= split_dot(dot_nt, distant, panel)
            inv_ref[rest, pl.ds(0, end)] -= split_dot(dot_nn, panel, inv_ref[span(b), pl.ds(0, end)])


D = 7168
FF = 18432
TILE = 128
decay_rate = 0.95
step_size = 0.3
epsilon = 1e-06

DP = 32
TENSOR = 16
CHIPS = 16
SLAB = RANK // DP
MESH = pl.DeviceIdType.MESH
VMEM = pl.BlockSpec(memory_space=pltpu.VMEM)
ANY = pl.BlockSpec(memory_space=pl.ANY)


def remote(src, dst, send, recv, dp, tensor):
    return pltpu.make_async_remote_copy(
        src_ref=src, dst_ref=dst, send_sem=send, recv_sem=recv, device_id=(dp, tensor), device_id_type=MESH
    )


def slab_rows(dp):
    return pl.ds(pl.multiple_of(SLAB * (CHIPS * lax.rem(dp, 2) + dp // 2), SLAB), SLAB)


LONG = CHIPS // 2


def spread_slabs(slab, dp, tensor, recv, ring_send, cross_send, pass_send, pass_recv):
    core, chip = lax.rem(dp, 2), dp // 2
    side, z = chip // LONG, lax.rem(chip, LONG)
    other = dp + 1 - 2 * core
    started = []

    def at(which_side, offset):
        return LONG * which_side + lax.rem(z + offset + LONG, LONG)

    def mine(source):
        return slab(2 * source + core)

    def send(source, target, sem):
        copy = remote(mine(source), mine(source), sem, recv.at[source], 2 * target + core, tensor)
        copy.start()
        started.append(copy)

    def hand_over(source):
        copy = remote(mine(source), mine(source), pass_send.at[source], pass_recv.at[source], other, tensor)
        copy.start()
        started.append(copy)

    def arrived(source):
        remote(mine(source), mine(source), ring_send.at[0], recv.at[source], other, tensor).wait_recv()

    across = at(1 - side, 0)
    offsets = [4, 3, -3, 2, -2, 1, -1]
    for offset in offsets:
        send(chip, at(side, offset), ring_send.at[offset % LONG])
    send(chip, across, cross_send.at[0])
    hand_over(chip)
    for offset in reversed(offsets):
        source = at(side, offset)
        arrived(source)
        send(source, across, cross_send.at[offset % LONG])
        hand_over(source)
    for offset in [0] + offsets[::-1]:
        source = at(1 - side, offset)
        arrived(source)
        hand_over(source)

    def passed(step, carry):
        source = lax.rem(chip + step, CHIPS)
        there = slab(2 * source + 1 - core)
        remote(there, there, pass_send.at[source], pass_recv.at[source], other, tensor).wait_recv()
        return carry

    lax.fori_loop(0, CHIPS, passed, 0)
    return started


OWNERS = 5
TALL = RANK // 8
WIDE_ROWS, WIDE_COLUMNS = 64, 128


CHUNK = 48
ROWS_OUT = FF // TENSOR // DP
COLUMNS_OUT = D // DP // TENSOR
TURN = 32


def step_kernel(weight_in, momentum_in, gradient_in, basis_in,
                new_momentum, new_basis, row_values, row_scales, column_values, column_scales,
                weight, momentum, gradient, basis, high, low, basis_high, basis_low, pair_out, pair_in, part, inbox, proj,
                gram, work, inverse, gram_part, gram_inbox, wide_part, wide_inbox, wide_all,
                back_high, fresh_high, fresh_low, ortho_high, ortho_low, square_inbox, update, turned, flipped,
                row_out, row_in, column_out, column_in, load, pair_send, pair_recv, send, recv,
                tile_send, tile_recv, back_send, back_recv, wide_send, wide_recv, out_send, out_recv,
                square_send, square_recv, row_send, row_recv, column_send, column_recv, *gather_sems):
    proj_sems, gram_sems = gather_sems[:len(gather_sems) // 2], gather_sems[len(gather_sems) // 2:]
    dp, tensor = lax.axis_index("dp"), lax.axis_index("tensor")
    core, chip = lax.rem(dp, 2), dp // 2
    other = dp + 1 - 2 * core
    half = RANK // 2
    rows, columns = momentum.shape
    width = columns // 3

    loads = [
        pltpu.make_async_copy(source, target, load.at[i])
        for i, (source, target) in enumerate(
            [(basis_in, basis), (gradient_in, gradient), (momentum_in, momentum), (weight_in, weight)]
        )
    ]
    for copy in loads:
        copy.start()
    barrier = pltpu.get_barrier_semaphore()

    def greet_rows(step, carry):
        pl.semaphore_signal(barrier, inc=1, device_id=(lax.rem(dp + step, DP), tensor), device_id_type=MESH)
        return carry

    def greet_columns(step, carry):
        pl.semaphore_signal(barrier, inc=1, device_id=(dp, lax.rem(tensor + step, TENSOR)), device_id_type=MESH)
        return carry

    lax.fori_loop(1, DP, greet_rows, 0)
    lax.fori_loop(1, TENSOR, greet_columns, 0)

    loads[0].wait()
    basis_high[...], basis_low[...] = halves(jnp.transpose(basis[...]))
    loads[1].wait()
    loads[2].wait()

    def product(first, j):
        span = pl.ds(j * width, width)
        rows = pl.ds(pl.multiple_of(first, half), half)
        return (
            dot_nn(basis_high[rows, :], high[:, span])
            + dot_nn(basis_high[rows, :], low[:, span])
            + dot_nn(basis_low[rows, :], high[:, span])
        )

    swaps = [remote(pair_out.at[j], pair_in.at[j], pair_send.at[j], pair_recv.at[j], other, tensor) for j in range(3)]
    for j in range(3):
        span = pl.ds(j * width, width)
        high[:, span], low[:, span] = halves(momentum[:, span] + gradient[:, span].astype(jnp.float32))
        pair_out[j] = product((1 - core) * half, j)
        if j == 0:
            pl.semaphore_wait(barrier, DP + TENSOR - 2)
        swaps[j].start()
    mine = [product(core * half, j) for j in range(3)]
    for j in range(3):
        swaps[j].wait_recv()
        part[:, pl.ds(j * width, width)] = (mine[j] + pair_in[j]).astype(jnp.bfloat16)

    def slab(which):
        return part.at[pl.ds(pl.multiple_of(which * SLAB, SLAB), SLAB), :]

    def slab_copy(step):
        to = lax.rem(chip + step, CHIPS)
        return remote(slab(to), inbox.at[chip], send.at[step], recv.at[chip], 2 * to + core, tensor)

    def slab_begin(step, carry):
        slab_copy(step).start()
        return carry

    def slab_arrive(step, total):
        source = lax.rem(chip + CHIPS - step, CHIPS)
        remote(inbox.at[source], inbox.at[source], send.at[0], recv.at[source], other, tensor).wait_recv()
        return total + inbox[source].astype(jnp.float32)

    def slab_drain(step, carry):
        slab_copy(step).wait_send()
        return carry

    lax.fori_loop(1, CHIPS, slab_begin, 0)
    column_out[...] = jnp.zeros(column_out.shape, jnp.bfloat16)
    row_out[...] = jnp.zeros(row_out.shape, jnp.bfloat16)
    total = part[pl.ds(pl.multiple_of(chip * SLAB, SLAB), SLAB), :].astype(jnp.float32)
    total = lax.fori_loop(1, CHIPS, slab_arrive, total)
    proj[slab_rows(dp), :] = total.astype(jnp.bfloat16)
    proj_sends = spread_slabs(lambda which: proj.at[slab_rows(which), :], dp, tensor, *proj_sems)

    def tile_row(which):
        both = dot_nt(proj[pl.ds(pl.multiple_of(16 * (which // 2), 16), 16), :], proj[...])
        return jnp.where(lax.rem(which, 2) == 0, both[:8], both[8:])

    upper, lower = tile_row(dp), tile_row(TALL - 1 - dp)
    column = lambda x, j: x[:, BLOCK * j:BLOCK * (j + 1)]
    short = dp < TALL // 4
    gram_part[0] = column(upper, 0)
    gram_part[1] = jnp.where(short, column(lower, 0), column(upper, 1))
    for j in range(2, OWNERS):
        gram_part[j] = jnp.where(short, column(lower, j - 1), column(lower, j - 2))

    def tile_copy(owner):
        return remote(gram_part.at[owner], gram_inbox.at[tensor], tile_send.at[owner], tile_recv.at[tensor], dp, owner)

    def tile_begin(owner, carry):
        @pl.when(owner != tensor)
        def _():
            tile_copy(owner).start()

        return carry

    lax.fori_loop(0, OWNERS, tile_begin, 0)
    work[:rows, :] = dot_nt(high[...], proj[...])

    def back_copy(step):
        to = lax.rem(tensor + step, TENSOR)
        here = gram.at[dp, tensor]
        return remote(here, here, back_send.at[step], back_recv.at[tensor], dp, to)

    @pl.when(tensor < OWNERS)
    def _():
        def arrive(step, total):
            source = lax.rem(tensor + step, TENSOR)
            there = gram_inbox.at[source]
            remote(there, there, tile_send.at[0], tile_recv.at[source], dp, tensor).wait_recv()
            return total + gram_inbox[source]

        def back_begin(step, carry):
            back_copy(step).start()
            return carry

        gram[dp, tensor] = lax.fori_loop(1, TENSOR, arrive, gram_part[tensor])
        lax.fori_loop(1, TENSOR, back_begin, 0)

    wide_part[:rows, :] = (work[:rows, :] + dot_nt(low[...], proj[...])).astype(jnp.bfloat16)
    wide_part[rows:, :] = jnp.zeros((wide_part.shape[0] - rows, RANK), jnp.bfloat16)

    def piece(ref, which):
        return ref.at[
            pl.ds(pl.multiple_of(WIDE_ROWS * (which // 4), WIDE_ROWS), WIDE_ROWS),
            pl.ds(pl.multiple_of(WIDE_COLUMNS * lax.rem(which, 4), WIDE_COLUMNS), WIDE_COLUMNS),
        ]

    def wide_copy(step):
        to = lax.rem(tensor + step, TENSOR)
        return remote(piece(wide_part, to), wide_inbox.at[tensor], wide_send.at[step], wide_recv.at[tensor], dp, to)

    def wide_begin(step, carry):
        wide_copy(step).start()
        return carry

    lax.fori_loop(1, TENSOR, wide_begin, 0)

    def wide_arrive(step, total):
        source = lax.rem(tensor + step, TENSOR)
        there = wide_inbox.at[source]
        remote(there, there, wide_send.at[0], wide_recv.at[source], dp, tensor).wait_recv()
        return total + wide_inbox[source].astype(jnp.float32)

    def out_copy(step):
        to = lax.rem(tensor + step, TENSOR)
        here = piece(wide_all, tensor)
        return remote(here, here, out_send.at[step], out_recv.at[tensor], dp, to)

    def out_begin(step, carry):
        out_copy(step).start()
        return carry

    def back_arrive(owner, carry):
        @pl.when(owner != tensor)
        def _():
            there = gram.at[dp, owner]
            remote(there, there, back_send.at[0], back_recv.at[owner], dp, tensor).wait_recv()

        return carry

    lax.fori_loop(0, OWNERS, back_arrive, 0)
    gram_sends = spread_slabs(lambda which: gram.at[which], dp, tensor, *gram_sems)
    work[...] = jnp.zeros_like(work)
    for i in range(DP):
        places = [(r, j) for r in (i, TALL - 1 - i) for j in range(8 * r // BLOCK + 1)]
        for j, (r, c) in enumerate(places):
            work[pl.ds(8 * r, 8), pl.ds(BLOCK * c, BLOCK)] = gram[i, j]
    piece(wide_all, tensor)[...] = lax.fori_loop(
        1, TENSOR, wide_arrive, piece(wide_part, tensor)[...].astype(jnp.float32)
    )
    lax.fori_loop(1, TENSOR, out_begin, 0)
    factor_and_invert(inverse, work)

    def out_arrive(step, carry):
        source = lax.rem(tensor + step, TENSOR)
        there = piece(wide_all, source)
        remote(there, there, out_send.at[0], out_recv.at[source], dp, tensor).wait_recv()
        return carry

    lax.fori_loop(1, TENSOR, out_arrive, 0)

    inverse_high, inverse_low = halves(inverse[...])
    wide_high, wide_low = halves(wide_all[:rows, :])
    back = dot_nt(wide_high, inverse_high) + dot_nt(wide_low, inverse_high) + dot_nt(wide_high, inverse_low)
    squares = jnp.sum(jnp.sum((back * back).reshape(rows // 8, 8, RANK), axis=0), axis=0, keepdims=True)
    lanes = RANK // 4
    square_inbox[dp] = jnp.concatenate(
        [squares[:, j * lanes:(j + 1) * lanes] for j in range(4)] + [jnp.zeros((4, lanes), jnp.float32)], axis=0
    )

    def square_copy(step):
        here = square_inbox.at[dp]
        return remote(here, here, square_send.at[step], square_recv.at[dp], lax.rem(dp + step, DP), tensor)

    def square_begin(step, carry):
        square_copy(step).start()
        return carry

    lax.fori_loop(1, DP, square_begin, 0)
    back_high[...] = back.astype(jnp.bfloat16)
    for j in range(3):
        span = pl.ds(j * width, width)
        ortho = dot_nn(inverse_high, proj[:, span]) + dot_nn(inverse_low, proj[:, span])
        ortho_high[:, span], ortho_low[:, span] = halves(ortho)

    def square_arrive(step, carry):
        source = lax.rem(dp + step, DP)
        there = square_inbox.at[source]
        remote(there, there, square_send.at[0], square_recv.at[source], dp, tensor).wait_recv()
        return carry

    lax.fori_loop(1, DP, square_arrive, 0)
    total = square_inbox[0]
    for source in range(1, DP):
        total += square_inbox[source]
    colsq = jnp.concatenate([total[j:j + 1, :] for j in range(4)], axis=1)
    fresh = back / jnp.sqrt(colsq + epsilon)
    new_basis[...] = fresh
    fresh_high[...], fresh_low[...] = halves(fresh)

    loads[3].wait()

    factor = step_size * math.sqrt(FF / D)
    shift = lax.rem(3 * dp, 4)
    for j in range(3):
        span = pl.ds(j * width, width)
        product = (
            dot_nn(fresh_high[...], ortho_high[:, span])
            + dot_nn(fresh_low[...], ortho_high[:, span])
            + dot_nn(fresh_high[...], ortho_low[:, span])
        )
        update[:, span] = weight[:, span].astype(jnp.float32) - factor * product

    def row_copy(step):
        to = lax.rem(dp + step, DP)
        return remote(row_out.at[to], row_in.at[dp], row_send.at[step], row_recv.at[dp], to, tensor)

    def column_copy(step):
        to = lax.rem(tensor + step, TENSOR)
        return remote(column_out.at[to], column_in.at[tensor], column_send.at[step], column_recv.at[tensor], dp, to)

    def row_begin(step, carry):
        row_copy(step).start()
        return carry

    def column_begin(step, carry):
        column_copy(step).start()
        return carry

    pieces = rows // TURN
    for i in range(pieces + 1):
        to = pl.ds(pl.multiple_of(TURN * lax.rem(i + shift, pieces + 1), TURN), TURN)
        turned[to, :] = update[pl.ds(TURN * i, TURN), :] if i < pieces else jnp.zeros((TURN, columns), jnp.float32)
    for to in range(TENSOR):
        column_out[to, pl.ds(0, COLUMNS_OUT), :] = update[pl.ds(COLUMNS_OUT * to, COLUMNS_OUT), :].astype(jnp.bfloat16)
    lax.fori_loop(1, TENSOR, column_begin, 0)
    for j in range(columns // TILE):
        flipped[pl.ds(TILE * j, TILE), :] = jnp.transpose(turned[:, pl.ds(TILE * j, TILE)])
    for to in range(DP):
        row_out[to, pl.ds(0, ROWS_OUT), :] = flipped[pl.ds(ROWS_OUT * to, ROWS_OUT), :].astype(jnp.bfloat16)
    lax.fori_loop(1, DP, row_begin, 0)
    column_in[tensor] = column_out[tensor]
    row_in[dp] = row_out[dp]

    for j in range(3):
        span = pl.ds(j * width, width)
        product = dot_nn(back_high[...], ortho_high[:, span])
        new_momentum[:, span] = momentum[:, span] + gradient[:, span].astype(jnp.float32) - (1.0 - decay_rate) * product

    def scaled(tile):
        largest = jnp.max(jnp.abs(tile), axis=1, keepdims=True)
        return (tile * (1.0 / (largest + epsilon))).astype(jnp.bfloat16), largest

    def column_quantize(step, scales):
        source = lax.rem(tensor + step, TENSOR)
        there = column_in.at[source]

        @pl.when(step > 0)
        def _():
            remote(there, there, column_send.at[0], column_recv.at[source], dp, tensor).wait_recv()

        lane_of = lax.broadcasted_iota(jnp.int32, scales.shape, 1)
        for j in range(columns // TILE):
            values, largest = scaled(column_in[source, :, pl.ds(TILE * j, TILE)].astype(jnp.float32))
            column_values[:, pl.ds(pl.multiple_of(columns * source + TILE * j, TILE), TILE)] = values[:COLUMNS_OUT]
            scales = jnp.where(lane_of == columns // TILE * source + j, largest, scales)
        return scales

    scales = lax.fori_loop(0, TENSOR, column_quantize, jnp.zeros((16, 2 * TILE), jnp.float32))
    column_scales[...] = scales[:COLUMNS_OUT, :FF // TILE]

    def row_quantize(step, scales):
        group = lax.rem(dp // 4 + (1 - 2 * lax.rem(step, 2)) * ((step + 1) // 2) + DP // 4, DP // 4)
        first = pl.multiple_of(4 * rows * group, TILE)
        lane_of = lax.broadcasted_iota(jnp.int32, scales.shape, 1)
        for i in range(4):
            source = 4 * group + i

            @pl.when(source != dp)
            def _():
                there = row_in.at[source]
                remote(there, there, row_send.at[0], row_recv.at[source], dp, tensor).wait_recv()

        for tile in range(4 * rows // TILE):
            which = TILE * tile // rows
            take = lambda i: row_in[4 * group + i, :, pl.ds(TILE * ((tile - rows * i // TILE) % 2), TILE)].astype(jnp.float32)
            block = take(which)
            bound = rows * (which + 1) - TILE * tile
            if bound < TILE:
                block = jnp.where(lane_of < bound, block, take(which + 1))
            values, largest = scaled(block)
            row_values[:, pl.ds(pl.multiple_of(first + TILE * tile, TILE), TILE)] = values[:ROWS_OUT]
            scales = jnp.where(lane_of == 4 * rows // TILE * group + tile, largest, scales)
        return scales

    scales = lax.fori_loop(0, DP // 4, row_quantize, jnp.zeros((CHUNK, TILE), jnp.float32))
    row_scales[...] = scales[:ROWS_OUT, :D // TILE]

    def tile_drain(owner, carry):
        @pl.when(owner != tensor)
        def _():
            tile_copy(owner).wait_send()

        return carry

    def drain(step, carry):
        wide_copy(step).wait_send()
        out_copy(step).wait_send()

        @pl.when(tensor < OWNERS)
        def _():
            back_copy(step).wait_send()

        return carry

    for copy in proj_sends + gram_sends:
        copy.wait_send()
    for copy in swaps:
        copy.wait_send()
    lax.fori_loop(1, CHIPS, slab_drain, 0)
    lax.fori_loop(0, OWNERS, tile_drain, 0)
    lax.fori_loop(1, TENSOR, drain, 0)

    def square_drain(step, carry):
        square_copy(step).wait_send()
        row_copy(step).wait_send()
        return carry

    def column_drain(step, carry):
        column_copy(step).wait_send()
        return carry

    lax.fori_loop(1, DP, square_drain, 0)
    lax.fori_loop(1, TENSOR, column_drain, 0)


def step(weight, momentum, gradient, basis):
    rows, columns = weight.shape
    half = RANK // 2
    padded = TENSOR // 4 * WIDE_ROWS
    dma = pltpu.SemaphoreType.DMA
    f32, bf16 = jnp.float32, jnp.bfloat16
    shape, vmem = jax.ShapeDtypeStruct, pltpu.VMEM
    gather = [dma((CHIPS,)), dma((LONG,)), dma((LONG,)), dma((CHIPS,)), dma((CHIPS,))]
    return pl.pallas_call(
        step_kernel,
        out_shape=(
            shape((rows, columns), f32),
            shape((rows, RANK), f32),
            shape((ROWS_OUT, D), bf16),
            shape((ROWS_OUT, D // TILE), f32),
            shape((COLUMNS_OUT, FF), bf16),
            shape((COLUMNS_OUT, FF // TILE), f32),
        ),
        in_specs=[ANY] * 4,
        out_specs=(VMEM,) * 6,
        scratch_shapes=[
            vmem((rows, columns), bf16),
            vmem((rows, columns), f32),
            vmem((rows, columns), bf16),
            vmem((rows, RANK), f32),
            vmem((rows, columns), bf16),
            vmem((rows, columns), bf16),
            vmem((RANK, rows), bf16),
            vmem((RANK, rows), bf16),
            vmem((3, half, columns // 3), f32),
            vmem((3, half, columns // 3), f32),
            vmem((half, columns), bf16),
            vmem((CHIPS, SLAB, columns), bf16),
            vmem((RANK, columns), bf16),
            vmem((DP, OWNERS, 8, BLOCK), f32),
            vmem((RANK, RANK), f32),
            vmem((RANK, RANK), f32),
            vmem((OWNERS, 8, BLOCK), f32),
            vmem((TENSOR, 8, BLOCK), f32),
            vmem((padded, RANK), bf16),
            vmem((TENSOR, WIDE_ROWS, WIDE_COLUMNS), bf16),
            vmem((padded, RANK), f32),
            vmem((rows, RANK), bf16),
            vmem((rows, RANK), bf16),
            vmem((rows, RANK), bf16),
            vmem((RANK, columns), bf16),
            vmem((RANK, columns), bf16),
            vmem((DP, 8, RANK // 4), f32),
            vmem((rows, columns), f32),
            vmem((rows + TURN, columns), f32),
            vmem((columns, rows + TURN), f32),
            vmem((DP, CHUNK, rows + TURN), bf16),
            vmem((DP, CHUNK, rows + TURN), bf16),
            vmem((TENSOR, 16, columns), bf16),
            vmem((TENSOR, 16, columns), bf16),
            dma((4,)), dma((3,)), dma((3,)), dma((CHIPS,)), dma((CHIPS,)),
            dma((OWNERS,)), dma((TENSOR,)), dma((TENSOR,)), dma((OWNERS,)),
            dma((TENSOR,)), dma((TENSOR,)), dma((TENSOR,)), dma((TENSOR,)),
            dma((DP,)), dma((DP,)), dma((DP,)), dma((DP,)), dma((TENSOR,)), dma((TENSOR,)),
        ] + gather + gather,
        compiler_params=pltpu.CompilerParams(collective_id=0, has_side_effects=True, vmem_limit_bytes=56 << 20),
    )(weight, momentum, gradient, basis)


def on_device(weight, gradient, momentum, basis):
    return step(weight, momentum, gradient, basis)


def solution(mesh):
    placed = (P("dp", "tensor"), P("dp", "tensor"), P("dp", "tensor"), P("dp", None))
    return jax.shard_map(
        on_device,
        mesh=mesh,
        in_specs=placed,
        out_specs=(
            P("dp", "tensor"),
            P("dp", None),
            P(("tensor", "dp"), None),
            P(("tensor", "dp"), None),
            P(("dp", "tensor"), None),
            P(("dp", "tensor"), None),
        ),
        check_vma=False,
    )
```

```python
import math

import jax
import jax.numpy as jnp
from jax import lax
from jax.experimental import pallas as pl
from jax.experimental.pallas import tpu as pltpu
from jax.sharding import PartitionSpec as P

RANK = 512
BLOCK = 128
STRIP = 8


def dot_nt(a, b):
    return lax.dot_general(a, b, (((1,), (1,)), ((), ())), preferred_element_type=jnp.float32)


def dot_nn(a, b):
    return lax.dot_general(a, b, (((1,), (0,)), ((), ())), preferred_element_type=jnp.float32)


def invert_block(tiles):
    shape = (STRIP, BLOCK)
    count = BLOCK // STRIP
    row_of = lax.broadcasted_iota(jnp.int32, shape, 0)
    lane_of = lax.broadcasted_iota(jnp.int32, shape, 1)
    tiles = list(tiles)
    own = [jnp.where(lane_of == row_of + STRIP * i, 1.0, 0.0).astype(jnp.float32) for i in range(count)]
    for s in range(count):
        spread = lambda tile, m, lane: jnp.broadcast_to(tile[m:m + 1, lane:lane + 1], shape)
        small = [[spread(tiles[s], m, STRIP * s + k) for k in range(m + 1)] for m in range(STRIP)]
        rows = [jnp.broadcast_to(tiles[s][m:m + 1, :], shape) for m in range(STRIP)]
        extra = [jnp.broadcast_to(own[s][m:m + 1, :], shape) for m in range(STRIP)]
        factor = [[None] * STRIP for _ in range(STRIP)]
        inverse, root = [], []
        for k in range(STRIP):
            root.append(lax.rsqrt(small[k][k]))
            inverse.append(1.0 / small[k][k])
            for m in range(k + 1, STRIP):
                f = small[m][k] * inverse[k]
                factor[m][k] = f
                for j in range(k + 1, m + 1):
                    small[m][j] = small[m][j] - (small[m][k] * small[j][k]) * inverse[k]
                rows[m] = rows[m] - f * rows[k]
                extra[m] = extra[m] - f * extra[k]
        for i in range(s + 1, count):
            cols = [jnp.broadcast_to(tiles[i][:, STRIP * s + k:STRIP * s + k + 1], shape) for k in range(STRIP)]
            for k in range(STRIP):
                for m in range(k + 1, STRIP):
                    cols[m] = cols[m] - cols[k] * factor[m][k]
            for k in range(STRIP):
                g = cols[k] * inverse[k]
                tiles[i] = tiles[i] - g * rows[k]
                own[i] = own[i] - g * extra[k]
        done = extra[0] * root[0]
        for m in range(1, STRIP):
            done = jnp.where(row_of == m, extra[m] * root[m], done)
        own[s] = done
    return own


def halves(x):
    high = x.astype(jnp.bfloat16)
    return high, (x - high.astype(jnp.float32)).astype(jnp.bfloat16)


def split_dot(dot, a, b):
    a_high, a_low = halves(a)
    b_high, b_low = halves(b)
    return dot(a_high, b_high) + (dot(a_high, b_low) + dot(a_low, b_high))


def factor_and_invert(inv_ref, a_ref):
    rank = a_ref.shape[0]
    blocks = rank // BLOCK
    span = lambda b: pl.ds(b * BLOCK, BLOCK)
    inv_ref[...] = jnp.zeros_like(inv_ref)
    diagonal = a_ref[span(0), span(0)]
    for b in range(blocks):
        inverse = jnp.concatenate(invert_block([diagonal[STRIP * i:STRIP * (i + 1)] for i in range(BLOCK // STRIP)]), axis=0)
        done, end = pl.ds(0, b * BLOCK), (b + 1) * BLOCK
        rest = pl.ds(end, rank - end)
        if b + 1 < blocks:
            near = split_dot(dot_nt, a_ref[span(b + 1), span(b)], inverse)
            diagonal = a_ref[span(b + 1), span(b + 1)] - split_dot(dot_nt, near, near)
        inv_ref[span(b), span(b)] = inverse
        if b:
            inv_ref[span(b), done] = split_dot(dot_nn, inverse, inv_ref[span(b), done])
        if b + 1 < blocks:
            panel = near
            if b + 2 < blocks:
                far = pl.ds(end + BLOCK, rank - end - BLOCK)
                distant = split_dot(dot_nt, a_ref[far, span(b)], inverse)
                panel = jnp.concatenate([near, distant], axis=0)
                a_ref[far, rest] -= split_dot(dot_nt, distant, panel)
            inv_ref[rest, pl.ds(0, end)] -= split_dot(dot_nn, panel, inv_ref[span(b), pl.ds(0, end)])


D = 7168
FF = 18432
TILE = 128
decay_rate = 0.95
step_size = 0.3
epsilon = 1e-06

DP = 32
TENSOR = 16
CHIPS = 16
SLAB = RANK // DP
MESH = pl.DeviceIdType.MESH
VMEM = pl.BlockSpec(memory_space=pltpu.VMEM)
ANY = pl.BlockSpec(memory_space=pl.ANY)


def remote(src, dst, send, recv, dp, tensor):
    return pltpu.make_async_remote_copy(
        src_ref=src, dst_ref=dst, send_sem=send, recv_sem=recv, device_id=(dp, tensor), device_id_type=MESH
    )


def slab_rows(dp):
    return pl.ds(pl.multiple_of(SLAB * (CHIPS * lax.rem(dp, 2) + dp // 2), SLAB), SLAB)


LONG = CHIPS // 2


def spread_slabs(slab, dp, tensor, recv, ring_send, cross_send, pass_send, pass_recv):
    core, chip = lax.rem(dp, 2), dp // 2
    side, z = chip // LONG, lax.rem(chip, LONG)
    other = dp + 1 - 2 * core
    started = []

    def at(which_side, offset):
        return LONG * which_side + lax.rem(z + offset + LONG, LONG)

    def mine(source):
        return slab(2 * source + core)

    def send(source, target, sem):
        copy = remote(mine(source), mine(source), sem, recv.at[source], 2 * target + core, tensor)
        copy.start()
        started.append(copy)

    def hand_over(source):
        copy = remote(mine(source), mine(source), pass_send.at[source], pass_recv.at[source], other, tensor)
        copy.start()
        started.append(copy)

    def arrived(source):
        remote(mine(source), mine(source), ring_send.at[0], recv.at[source], other, tensor).wait_recv()

    across = at(1 - side, 0)
    offsets = [4, 3, -3, 2, -2, 1, -1]
    for offset in offsets:
        send(chip, at(side, offset), ring_send.at[offset % LONG])
    send(chip, across, cross_send.at[0])
    hand_over(chip)
    for offset in reversed(offsets):
        source = at(side, offset)
        arrived(source)
        send(source, across, cross_send.at[offset % LONG])
        hand_over(source)
    for offset in [0] + offsets[::-1]:
        source = at(1 - side, offset)
        arrived(source)
        hand_over(source)

    def passed(step, carry):
        source = lax.rem(chip + step, CHIPS)
        there = slab(2 * source + 1 - core)
        remote(there, there, pass_send.at[source], pass_recv.at[source], other, tensor).wait_recv()
        return carry

    lax.fori_loop(0, CHIPS, passed, 0)
    return started


OWNERS = 5
TALL = RANK // 8
WIDE_ROWS, WIDE_COLUMNS = 64, 128


CHUNK = 48
ROWS_OUT = FF // TENSOR // DP
COLUMNS_OUT = D // DP // TENSOR
TURN = 32


def step_kernel(weight_in, momentum_in, gradient_in, basis_in,
                new_momentum, new_basis, row_values, row_scales, column_values, column_scales,
                weight, momentum, gradient, basis, high, low, basis_high, basis_low, pair_out, pair_in, part, inbox, proj,
                gram, work, inverse, gram_part, gram_inbox, wide_part, wide_inbox, wide_all,
                back_high, fresh_high, fresh_low, ortho_high, ortho_low, square_inbox, update, turned, flipped,
                row_out, row_in, column_out, column_in, load, pair_send, pair_recv, send, recv,
                tile_send, tile_recv, back_send, back_recv, wide_send, wide_recv, out_send, out_recv,
                square_send, square_recv, row_send, row_recv, column_send, column_recv, *gather_sems):
    proj_sems, gram_sems = gather_sems[:len(gather_sems) // 2], gather_sems[len(gather_sems) // 2:]
    dp, tensor = lax.axis_index("dp"), lax.axis_index("tensor")
    core, chip = lax.rem(dp, 2), dp // 2
    other = dp + 1 - 2 * core
    half = RANK // 2
    rows, columns = momentum.shape
    width = columns // 3

    loads = [
        pltpu.make_async_copy(source, target, load.at[i])
        for i, (source, target) in enumerate(
            [(basis_in, basis), (gradient_in, gradient), (momentum_in, momentum), (weight_in, weight)]
        )
    ]
    for copy in loads:
        copy.start()
    barrier = pltpu.get_barrier_semaphore()

    def greet_rows(step, carry):
        pl.semaphore_signal(barrier, inc=1, device_id=(lax.rem(dp + step, DP), tensor), device_id_type=MESH)
        return carry

    def greet_columns(step, carry):
        pl.semaphore_signal(barrier, inc=1, device_id=(dp, lax.rem(tensor + step, TENSOR)), device_id_type=MESH)
        return carry

    lax.fori_loop(1, DP, greet_rows, 0)
    lax.fori_loop(1, TENSOR, greet_columns, 0)

    loads[0].wait()
    basis_high[...], basis_low[...] = halves(jnp.transpose(basis[...]))
    loads[1].wait()
    loads[2].wait()

    def product(first, j):
        span = pl.ds(j * width, width)
        rows = pl.ds(pl.multiple_of(first, half), half)
        return (
            dot_nn(basis_high[rows, :], high[:, span])
            + dot_nn(basis_high[rows, :], low[:, span])
            + dot_nn(basis_low[rows, :], high[:, span])
        )

    swaps = [remote(pair_out.at[j], pair_in.at[j], pair_send.at[j], pair_recv.at[j], other, tensor) for j in range(3)]
    for j in range(3):
        span = pl.ds(j * width, width)
        high[:, span], low[:, span] = halves(momentum[:, span] + gradient[:, span].astype(jnp.float32))
        pair_out[j] = product((1 - core) * half, j)
        if j == 0:
            pl.semaphore_wait(barrier, DP + TENSOR - 2)
        swaps[j].start()
    mine = [product(core * half, j) for j in range(3)]
    for j in range(3):
        swaps[j].wait_recv()
        part[:, pl.ds(j * width, width)] = (mine[j] + pair_in[j]).astype(jnp.bfloat16)

    def slab(which):
        return part.at[pl.ds(pl.multiple_of(which * SLAB, SLAB), SLAB), :]

    def slab_copy(step):
        to = lax.rem(chip + step, CHIPS)
        return remote(slab(to), inbox.at[chip], send.at[step], recv.at[chip], 2 * to + core, tensor)

    def slab_begin(step, carry):
        slab_copy(step).start()
        return carry

    def slab_arrive(step, total):
        source = lax.rem(chip + CHIPS - step, CHIPS)
        remote(inbox.at[source], inbox.at[source], send.at[0], recv.at[source], other, tensor).wait_recv()
        return total + inbox[source].astype(jnp.float32)

    def slab_drain(step, carry):
        slab_copy(step).wait_send()
        return carry

    lax.fori_loop(1, CHIPS, slab_begin, 0)
    column_out[...] = jnp.zeros(column_out.shape, jnp.bfloat16)
    row_out[...] = jnp.zeros(row_out.shape, jnp.bfloat16)
    total = part[pl.ds(pl.multiple_of(chip * SLAB, SLAB), SLAB), :].astype(jnp.float32)
    total = lax.fori_loop(1, CHIPS, slab_arrive, total)
    proj[slab_rows(dp), :] = total.astype(jnp.bfloat16)
    proj_sends = spread_slabs(lambda which: proj.at[slab_rows(which), :], dp, tensor, *proj_sems)

    def tile_row(which):
        both = dot_nt(proj[pl.ds(pl.multiple_of(16 * (which // 2), 16), 16), :], proj[...])
        return jnp.where(lax.rem(which, 2) == 0, both[:8], both[8:])

    upper, lower = tile_row(dp), tile_row(TALL - 1 - dp)
    column = lambda x, j: x[:, BLOCK * j:BLOCK * (j + 1)]
    short = dp < TALL // 4
    gram_part[0] = column(upper, 0)
    gram_part[1] = jnp.where(short, column(lower, 0), column(upper, 1))
    for j in range(2, OWNERS):
        gram_part[j] = jnp.where(short, column(lower, j - 1), column(lower, j - 2))

    def tile_copy(owner):
        return remote(gram_part.at[owner], gram_inbox.at[tensor], tile_send.at[owner], tile_recv.at[tensor], dp, owner)

    def tile_begin(owner, carry):
        @pl.when(owner != tensor)
        def _():
            tile_copy(owner).start()

        return carry

    lax.fori_loop(0, OWNERS, tile_begin, 0)
    work[:rows, :] = dot_nt(high[...], proj[...])

    def back_copy(step):
        to = lax.rem(tensor + step, TENSOR)
        here = gram.at[dp, tensor]
        return remote(here, here, back_send.at[step], back_recv.at[tensor], dp, to)

    @pl.when(tensor < OWNERS)
    def _():
        def arrive(step, total):
            source = lax.rem(tensor + step, TENSOR)
            there = gram_inbox.at[source]
            remote(there, there, tile_send.at[0], tile_recv.at[source], dp, tensor).wait_recv()
            return total + gram_inbox[source]

        def back_begin(step, carry):
            back_copy(step).start()
            return carry

        gram[dp, tensor] = lax.fori_loop(1, TENSOR, arrive, gram_part[tensor])
        lax.fori_loop(1, TENSOR, back_begin, 0)

    wide_part[:rows, :] = (work[:rows, :] + dot_nt(low[...], proj[...])).astype(jnp.bfloat16)
    wide_part[rows:, :] = jnp.zeros((wide_part.shape[0] - rows, RANK), jnp.bfloat16)

    def piece(ref, which):
        return ref.at[
            pl.ds(pl.multiple_of(WIDE_ROWS * (which // 4), WIDE_ROWS), WIDE_ROWS),
            pl.ds(pl.multiple_of(WIDE_COLUMNS * lax.rem(which, 4), WIDE_COLUMNS), WIDE_COLUMNS),
        ]

    def wide_copy(step):
        to = lax.rem(tensor + step, TENSOR)
        return remote(piece(wide_part, to), wide_inbox.at[tensor], wide_send.at[step], wide_recv.at[tensor], dp, to)

    def wide_begin(step, carry):
        wide_copy(step).start()
        return carry

    lax.fori_loop(1, TENSOR, wide_begin, 0)

    def wide_arrive(step, total):
        source = lax.rem(tensor + step, TENSOR)
        there = wide_inbox.at[source]
        remote(there, there, wide_send.at[0], wide_recv.at[source], dp, tensor).wait_recv()
        return total + wide_inbox[source].astype(jnp.float32)

    def out_copy(step):
        to = lax.rem(tensor + step, TENSOR)
        here = piece(wide_all, tensor)
        return remote(here, here, out_send.at[step], out_recv.at[tensor], dp, to)

    def out_begin(step, carry):
        out_copy(step).start()
        return carry

    def back_arrive(owner, carry):
        @pl.when(owner != tensor)
        def _():
            there = gram.at[dp, owner]
            remote(there, there, back_send.at[0], back_recv.at[owner], dp, tensor).wait_recv()

        return carry

    lax.fori_loop(0, OWNERS, back_arrive, 0)
    gram_sends = spread_slabs(lambda which: gram.at[which], dp, tensor, *gram_sems)
    work[...] = jnp.zeros_like(work)
    for i in range(DP):
        places = [(r, j) for r in (i, TALL - 1 - i) for j in range(8 * r // BLOCK + 1)]
        for j, (r, c) in enumerate(places):
            work[pl.ds(8 * r, 8), pl.ds(BLOCK * c, BLOCK)] = gram[i, j]
    piece(wide_all, tensor)[...] = lax.fori_loop(
        1, TENSOR, wide_arrive, piece(wide_part, tensor)[...].astype(jnp.float32)
    )
    lax.fori_loop(1, TENSOR, out_begin, 0)
    factor_and_invert(inverse, work)

    def out_arrive(step, carry):
        source = lax.rem(tensor + step, TENSOR)
        there = piece(wide_all, source)
        remote(there, there, out_send.at[0], out_recv.at[source], dp, tensor).wait_recv()
        return carry

    lax.fori_loop(1, TENSOR, out_arrive, 0)

    inverse_high, inverse_low = halves(inverse[...])
    wide_high, wide_low = halves(wide_all[:rows, :])
    back = dot_nt(wide_high, inverse_high) + dot_nt(wide_low, inverse_high) + dot_nt(wide_high, inverse_low)
    squares = jnp.sum(jnp.sum((back * back).reshape(rows // 8, 8, RANK), axis=0), axis=0, keepdims=True)
    lanes = RANK // 4
    square_inbox[dp] = jnp.concatenate(
        [squares[:, j * lanes:(j + 1) * lanes] for j in range(4)] + [jnp.zeros((4, lanes), jnp.float32)], axis=0
    )

    def square_copy(step):
        here = square_inbox.at[dp]
        return remote(here, here, square_send.at[step], square_recv.at[dp], lax.rem(dp + step, DP), tensor)

    def square_begin(step, carry):
        square_copy(step).start()
        return carry

    lax.fori_loop(1, DP, square_begin, 0)
    back_high[...] = back.astype(jnp.bfloat16)
    for j in range(3):
        span = pl.ds(j * width, width)
        ortho = dot_nn(inverse_high, proj[:, span]) + dot_nn(inverse_low, proj[:, span])
        ortho_high[:, span], ortho_low[:, span] = halves(ortho)

    def square_arrive(step, carry):
        source = lax.rem(dp + step, DP)
        there = square_inbox.at[source]
        remote(there, there, square_send.at[0], square_recv.at[source], dp, tensor).wait_recv()
        return carry

    lax.fori_loop(1, DP, square_arrive, 0)
    total = square_inbox[0]
    for source in range(1, DP):
        total += square_inbox[source]
    colsq = jnp.concatenate([total[j:j + 1, :] for j in range(4)], axis=1)
    fresh = back / jnp.sqrt(colsq + epsilon)
    new_basis[...] = fresh
    fresh_high[...], fresh_low[...] = halves(fresh)

    loads[3].wait()

    factor = step_size * math.sqrt(FF / D)
    shift = lax.rem(3 * dp, 4)
    for j in range(3):
        span = pl.ds(j * width, width)
        product = (
            dot_nn(fresh_high[...], ortho_high[:, span])
            + dot_nn(fresh_low[...], ortho_high[:, span])
            + dot_nn(fresh_high[...], ortho_low[:, span])
        )
        update[:, span] = weight[:, span].astype(jnp.float32) - factor * product

    def row_copy(step):
        to = lax.rem(dp + step, DP)
        return remote(row_out.at[to], row_in.at[dp], row_send.at[step], row_recv.at[dp], to, tensor)

    def column_copy(step):
        to = lax.rem(tensor + step, TENSOR)
        return remote(column_out.at[to], column_in.at[tensor], column_send.at[step], column_recv.at[tensor], dp, to)

    def row_begin(step, carry):
        row_copy(step).start()
        return carry

    def column_begin(step, carry):
        column_copy(step).start()
        return carry

    pieces = rows // TURN
    for i in range(pieces + 1):
        to = pl.ds(pl.multiple_of(TURN * lax.rem(i + shift, pieces + 1), TURN), TURN)
        turned[to, :] = update[pl.ds(TURN * i, TURN), :] if i < pieces else jnp.zeros((TURN, columns), jnp.float32)
    for to in range(TENSOR):
        column_out[to, pl.ds(0, COLUMNS_OUT), :] = update[pl.ds(COLUMNS_OUT * to, COLUMNS_OUT), :].astype(jnp.bfloat16)
    lax.fori_loop(1, TENSOR, column_begin, 0)
    for j in range(columns // TILE):
        flipped[pl.ds(TILE * j, TILE), :] = jnp.transpose(turned[:, pl.ds(TILE * j, TILE)])
    for to in range(DP):
        row_out[to, pl.ds(0, ROWS_OUT), :] = flipped[pl.ds(ROWS_OUT * to, ROWS_OUT), :].astype(jnp.bfloat16)
    lax.fori_loop(1, DP, row_begin, 0)
    column_in[tensor] = column_out[tensor]
    row_in[dp] = row_out[dp]

    for j in range(3):
        span = pl.ds(j * width, width)
        product = dot_nn(back_high[...], ortho_high[:, span])
        new_momentum[:, span] = momentum[:, span] + gradient[:, span].astype(jnp.float32) - (1.0 - decay_rate) * product

    def scaled(tile):
        largest = jnp.max(jnp.abs(tile), axis=1, keepdims=True)
        return (tile * (1.0 / (largest + epsilon))).astype(jnp.bfloat16), largest

    def column_quantize(step, scales):
        source = lax.rem(tensor + step, TENSOR)
        there = column_in.at[source]

        @pl.when(step > 0)
        def _():
            remote(there, there, column_send.at[0], column_recv.at[source], dp, tensor).wait_recv()

        lane_of = lax.broadcasted_iota(jnp.int32, scales.shape, 1)
        for j in range(columns // TILE):
            values, largest = scaled(column_in[source, :, pl.ds(TILE * j, TILE)].astype(jnp.float32))
            column_values[:, pl.ds(pl.multiple_of(columns * source + TILE * j, TILE), TILE)] = values[:COLUMNS_OUT]
            scales = jnp.where(lane_of == columns // TILE * source + j, largest, scales)
        return scales

    scales = lax.fori_loop(0, TENSOR, column_quantize, jnp.zeros((16, 2 * TILE), jnp.float32))
    column_scales[...] = scales[:COLUMNS_OUT, :FF // TILE]

    def row_quantize(step, scales):
        group = lax.rem(dp // 4 + (1 - 2 * lax.rem(step, 2)) * ((step + 1) // 2) + DP // 4, DP // 4)
        first = pl.multiple_of(4 * rows * group, TILE)
        lane_of = lax.broadcasted_iota(jnp.int32, scales.shape, 1)
        for i in range(4):
            source = 4 * group + i

            @pl.when(source != dp)
            def _():
                there = row_in.at[source]
                remote(there, there, row_send.at[0], row_recv.at[source], dp, tensor).wait_recv()

        for tile in range(4 * rows // TILE):
            which = TILE * tile // rows
            take = lambda i: row_in[4 * group + i, :, pl.ds(TILE * ((tile - rows * i // TILE) % 2), TILE)].astype(jnp.float32)
            block = take(which)
            bound = rows * (which + 1) - TILE * tile
            if bound < TILE:
                block = jnp.where(lane_of < bound, block, take(which + 1))
            values, largest = scaled(block)
            row_values[:, pl.ds(pl.multiple_of(first + TILE * tile, TILE), TILE)] = values[:ROWS_OUT]
            scales = jnp.where(lane_of == 4 * rows // TILE * group + tile, largest, scales)
        return scales

    scales = lax.fori_loop(0, DP // 4, row_quantize, jnp.zeros((CHUNK, TILE), jnp.float32))
    row_scales[...] = scales[:ROWS_OUT, :D // TILE]

    def tile_drain(owner, carry):
        @pl.when(owner != tensor)
        def _():
            tile_copy(owner).wait_send()

        return carry

    def drain(step, carry):
        wide_copy(step).wait_send()
        out_copy(step).wait_send()

        @pl.when(tensor < OWNERS)
        def _():
            back_copy(step).wait_send()

        return carry

    for copy in proj_sends + gram_sends:
        copy.wait_send()
    for copy in swaps:
        copy.wait_send()
    lax.fori_loop(1, CHIPS, slab_drain, 0)
    lax.fori_loop(0, OWNERS, tile_drain, 0)
    lax.fori_loop(1, TENSOR, drain, 0)

    def square_drain(step, carry):
        square_copy(step).wait_send()
        row_copy(step).wait_send()
        return carry

    def column_drain(step, carry):
        column_copy(step).wait_send()
        return carry

    lax.fori_loop(1, DP, square_drain, 0)
    lax.fori_loop(1, TENSOR, column_drain, 0)


def step(weight, momentum, gradient, basis):
    rows, columns = weight.shape
    half = RANK // 2
    padded = TENSOR // 4 * WIDE_ROWS
    dma = pltpu.SemaphoreType.DMA
    f32, bf16 = jnp.float32, jnp.bfloat16
    shape, vmem = jax.ShapeDtypeStruct, pltpu.VMEM
    gather = [dma((CHIPS,)), dma((LONG,)), dma((LONG,)), dma((CHIPS,)), dma((CHIPS,))]
    return pl.pallas_call(
        step_kernel,
        out_shape=(
            shape((rows, columns), f32),
            shape((rows, RANK), f32),
            shape((ROWS_OUT, D), bf16),
            shape((ROWS_OUT, D // TILE), f32),
            shape((COLUMNS_OUT, FF), bf16),
            shape((COLUMNS_OUT, FF // TILE), f32),
        ),
        in_specs=[ANY] * 4,
        out_specs=(VMEM,) * 6,
        scratch_shapes=[
            vmem((rows, columns), bf16),
            vmem((rows, columns), f32),
            vmem((rows, columns), bf16),
            vmem((rows, RANK), f32),
            vmem((rows, columns), bf16),
            vmem((rows, columns), bf16),
            vmem((RANK, rows), bf16),
            vmem((RANK, rows), bf16),
            vmem((3, half, columns // 3), f32),
            vmem((3, half, columns // 3), f32),
            vmem((half, columns), bf16),
            vmem((CHIPS, SLAB, columns), bf16),
            vmem((RANK, columns), bf16),
            vmem((DP, OWNERS, 8, BLOCK), f32),
            vmem((RANK, RANK), f32),
            vmem((RANK, RANK), f32),
            vmem((OWNERS, 8, BLOCK), f32),
            vmem((TENSOR, 8, BLOCK), f32),
            vmem((padded, RANK), bf16),
            vmem((TENSOR, WIDE_ROWS, WIDE_COLUMNS), bf16),
            vmem((padded, RANK), f32),
            vmem((rows, RANK), bf16),
            vmem((rows, RANK), bf16),
            vmem((rows, RANK), bf16),
            vmem((RANK, columns), bf16),
            vmem((RANK, columns), bf16),
            vmem((DP, 8, RANK // 4), f32),
            vmem((rows, columns), f32),
            vmem((rows + TURN, columns), f32),
            vmem((columns, rows + TURN), f32),
            vmem((DP, CHUNK, rows + TURN), bf16),
            vmem((DP, CHUNK, rows + TURN), bf16),
            vmem((TENSOR, 16, columns), bf16),
            vmem((TENSOR, 16, columns), bf16),
            dma((4,)), dma((3,)), dma((3,)), dma((CHIPS,)), dma((CHIPS,)),
            dma((OWNERS,)), dma((TENSOR,)), dma((TENSOR,)), dma((OWNERS,)),
            dma((TENSOR,)), dma((TENSOR,)), dma((TENSOR,)), dma((TENSOR,)),
            dma((DP,)), dma((DP,)), dma((DP,)), dma((DP,)), dma((TENSOR,)), dma((TENSOR,)),
        ] + gather + gather,
        compiler_params=pltpu.CompilerParams(collective_id=0, has_side_effects=True, vmem_limit_bytes=56 << 20),
    )(weight, momentum, gradient, basis)


def settle_kernel(*refs):
    sems, count = refs[-1], len(refs) // 2
    copies = [pltpu.make_async_copy(refs[i], refs[count + i], sems.at[i]) for i in range(count)]
    for copy in copies:
        copy.start()
    for copy in copies:
        copy.wait()


def settle(arrays):
    count = len(arrays)
    return pl.pallas_call(
        settle_kernel,
        out_shape=tuple(jax.ShapeDtypeStruct(x.shape, x.dtype) for x in arrays),
        in_specs=[VMEM] * count,
        out_specs=(ANY,) * count,
        scratch_shapes=[pltpu.SemaphoreType.DMA((count,))],
        compiler_params=pltpu.CompilerParams(vmem_limit_bytes=16 << 20),
    )(*arrays)


def on_device(weight, gradient, momentum, basis):
    return settle(step(weight, momentum, gradient, basis))


def solution(mesh):
    placed = (P("dp", "tensor"), P("dp", "tensor"), P("dp", "tensor"), P("dp", None))
    return jax.shard_map(
        on_device,
        mesh=mesh,
        in_specs=placed,
        out_specs=(
            P("dp", "tensor"),
            P("dp", None),
            P(("tensor", "dp"), None),
            P(("tensor", "dp"), None),
            P(("dp", "tensor"), None),
            P(("dp", "tensor"), None),
        ),
        check_vma=False,
    )
```
